128 devices in a mesh: row: 16 (over z, y), col: 8 (over x, core).
Axes of the slice: x: 4, y: 4, z: 4, core: 2. Of those that a mesh axis runs over, the one named last changes fastest.
Arguments:
- source_cells: float32 [32768, 64], P(('row', 'col')), may hold values from -6 to 6
- target_cells: float32 [16384, 64], P(('col', 'row')), may hold values from -6 to 6
- source_mass: float32 [32768], P(('row', 'col')), may hold values from 0.001 to 1000
- target_mass: float32 [16384], P(('col', 'row')), may hold values from 0.001 to 1000
- support: int32 [32, 16], P('row', 'col'), may hold values from 0 to 1, as said below
Outputs:
- source_potential: float32 [32768], P('row')
- target_potential: float32 [16384], P('col')
The draws below stay inside these ranges and needn't reach their ends.
Inputs may be any that keep to these rules, and one draw needn't show every extreme that they name: Every source block has at least one supported target block, and every target block has at least one supported source block; the support is uneven from block to block.
All inputs are finite; a program needn't handle non-finite values.
Results may differ from the reference program's by a relative error of at most 0.0003.
Values sent between devices are 32-bit elements; how exact they have to be, the bound alone decides.
A program may use at most 128 MiB of HBM per device.

```python
import math
import jax
import jax.numpy as jnp
from jax import lax

LATENT = 64
BLK = 1024
ITERS = 2
NSB = 32
NTB = 16
NS = 32768
NT = 16384


def draw_support(key, part):
    key = jax.random.fold_in(key, 11)
    key_perm, key_rate, key_roll = jax.random.split(key, 3)
    order = jax.random.permutation(key_perm, NTB)
    rows = jnp.arange(NSB)
    cols = jnp.arange(NTB)
    chosen = order[rows % NTB]
    sure = cols[None, :] == chosen[:, None]
    rate = jax.random.randint(key_rate, (NSB, 1), 0, 41)
    roll = jax.random.randint(key_roll, (NSB, NTB), 0, 100)
    return jnp.logical_or(sure, roll < rate).astype(jnp.int32)


def shard_levels(key, dims, pieces, low, high):
    level = 1.0
    for axis_at, shards_of in pieces:
        steps = jax.random.uniform(jax.random.fold_in(jax.random.fold_in(key, 6), axis_at), (shards_of,), jnp.float32, low / len(pieces), high / len(pieces))
        level = level * jnp.repeat(jnp.exp(steps), dims[axis_at] // shards_of).reshape((-1,) + (1,) * (len(dims) - 1 - axis_at))
    return level


def scatter_about(rng, extent, deviation, limit, cuts=(), kind=jnp.bfloat16):
    drawn = jax.random.normal(rng, extent, jnp.float32) * deviation
    if len(cuts) > 0:
        drawn = shard_levels(rng, extent, cuts, -0.22, 0.18) * drawn
    return jnp.clip(drawn, min=-limit, max=limit).astype(kind)


def setup_inputs(seed: int = 0) -> dict:
    seeds = jax.random.split(jax.random.key(seed), 6)
    source_cells = scatter_about(seeds[0], (NS, LATENT), 1.0, 6.0, ((0, 128),), jnp.float32)
    target_cells = scatter_about(seeds[1], (NT, LATENT), 1.0, 6.0, ((0, 128),), jnp.float32)
    source_mass = jnp.clip(jnp.exp(math.log(1000.0) - 13.815511 * jax.random.uniform(seeds[2], (NS,), jnp.float32) ** shard_levels(seeds[2], (NS,), ((0, 128),), -0.2, 0.2)), 0.001, 1000.0)
    target_mass = jnp.clip(jnp.exp(math.log(1000.0) - 13.815511 * jax.random.uniform(seeds[3], (NT,), jnp.float32) ** shard_levels(seeds[3], (NT,), ((0, 128),), -0.2, 0.2)), 0.001, 1000.0)
    support = draw_support(jax.random.fold_in(seeds[5], 71), 0)
    return {"source_cells": source_cells, "target_cells": target_cells, "source_mass": source_mass, "target_mass": target_mass, "support": support}


epsilon = 0.02
negative_fill = -1.0e30


def pair_cost(left, left_sq, right, right_sq):
    cross = jnp.dot(left, right.T, precision=lax.Precision.HIGHEST, preferred_element_type=jnp.float32)
    return (left_sq[:, None] + right_sq[None, :] - 2.0 * cross) / left.shape[1]


def sweep(rows_pts, rows_sq, rows_logm, cols_pts, cols_sq, cols_pot, mask):
    def per_row(args):
        pts, sq, logm, live_row = args

        def step(carry, inner):
            cpts, csq, cpot, live = inner

            def update(state):
                peak, total = state
                scores = cpot[None, :] - pair_cost(pts, sq, cpts, csq) / epsilon
                local_peak = jnp.max(scores, axis=1)
                local_total = jnp.sum(jnp.exp(scores - local_peak[:, None]), axis=1)
                top = jnp.maximum(peak, local_peak)
                return top, total * jnp.exp(peak - top) + local_total * jnp.exp(local_peak - top)

            return lax.cond(live == 1, update, lambda state: state, carry), None

        start = (jnp.full((pts.shape[0],), negative_fill, jnp.float32), jnp.zeros((pts.shape[0],), jnp.float32))
        (peak, total), unused = lax.scan(step, start, (cols_pts, cols_sq, cols_pot, live_row))
        return logm - (peak + jnp.log(total))

    return lax.map(per_row, (rows_pts, rows_sq, rows_logm, mask))


def reference(source_cells, target_cells, source_mass, target_mass, support):
    src = source_cells.reshape(NSB, BLK, LATENT)
    tgt = target_cells.reshape(NTB, BLK, LATENT)
    src_sq = jnp.sum(src * src, axis=2)
    tgt_sq = jnp.sum(tgt * tgt, axis=2)
    log_source = jnp.log(source_mass).reshape(NSB, BLK)
    log_target = jnp.log(target_mass).reshape(NTB, BLK)
    target_pot = jnp.zeros((NTB, BLK), jnp.float32)
    source_pot = jnp.zeros((NSB, BLK), jnp.float32)
    for step in range(ITERS):
        source_pot = sweep(src, src_sq, log_source, tgt, tgt_sq, target_pot, support)
        target_pot = sweep(tgt, tgt_sq, log_target, src, src_sq, source_pot, support.T)
    return (epsilon * source_pot).reshape(NS), (epsilon * target_pot).reshape(NT)
```

```python
import math

import jax
import jax.numpy as jnp
from jax import lax
from jax.experimental import pallas as pl
from jax.experimental.pallas import tpu as pltpu
from jax.sharding import PartitionSpec as P

MESH = pl.DeviceIdType.MESH
LATENT = 64
ROWS = 16
COLS = 8
LANES = 128
GROUPS = 16
EPSILON = 0.02
NEGATIVE = -1e30
SCALE = math.sqrt(2.0 * math.log2(math.e) / (LATENT * EPSILON))
BACK = EPSILON * math.log(2.0)


def pieces(value):
    high = value.astype(jnp.bfloat16)
    rest = value - high.astype(jnp.float32)
    mid = rest.astype(jnp.bfloat16)
    low = (rest - mid.astype(jnp.float32)).astype(jnp.bfloat16)
    return high, mid, low


def tree(op, parts):
    parts = list(parts)
    while len(parts) > 1:
        parts = [
            op(parts[k], parts[k + 1]) if k + 1 < len(parts) else parts[k]
            for k in range(0, len(parts), 2)
        ]
    return parts[0]


def kernel(
    x_ref, y_ref, a_ref, b_ref, support_ref, u_ref, v_ref,
    xbuf, ybuf, left, right, score, upart, vpart, ucol, vbias,
    peak_rows, total_rows,
    x_send, x_recv, y_send, y_recv, u_send, u_recv, v_send, v_recv,
):
    row = lax.axis_index("row")
    col = lax.axis_index("col")

    barrier = pltpu.get_barrier_semaphore()
    for k in range(1, COLS):
        pl.semaphore_signal(barrier, inc=1, device_id=(row, col ^ k), device_id_type=MESH)
    for k in range(1, ROWS):
        pl.semaphore_signal(barrier, inc=1, device_id=(row ^ k, col), device_id_type=MESH)

    def bias(a, b):
        return jnp.where(support_ref[a, b] == 1, jnp.float32(0.0), jnp.float32(NEGATIVE))

    y_cells = (y_ref[...] * SCALE).T
    ybuf[row, 0:LATENT, :] = y_cells
    ybuf[row, LATENT : LATENT + 1, :] = jnp.log2(b_ref[...])
    ybuf[row, LATENT + 1 : LATENT + 2, :] = 0.5 * jnp.sum(y_cells * y_cells, axis=0, keepdims=True)
    x_cells = x_ref[...] * SCALE
    xbuf[col, 0:LANES, 0:LATENT] = x_cells[0:LANES]
    xbuf[col, 0:LANES, LATENT : 2 * LATENT] = x_cells[LANES : 2 * LANES]
    x_turned = x_cells.T
    x_half = 0.5 * jnp.sum(x_turned * x_turned, axis=0, keepdims=True)
    xbuf[col, LANES : LANES + 2, :] = jnp.log2(a_ref[...])
    xbuf[col, LANES + 2 : LANES + 3, :] = x_half[:, 0:LANES]
    xbuf[col, LANES + 3 : LANES + 4, :] = x_half[:, LANES : 2 * LANES]

    pl.semaphore_wait(barrier, COLS + ROWS - 2)

    def over_row(ref, send, recv, k):
        return pltpu.make_async_remote_copy(
            src_ref=ref.at[row], dst_ref=ref.at[row], send_sem=send.at[k], recv_sem=recv.at[k],
            device_id=(row ^ k, col), device_id_type=MESH,
        )

    def over_col(ref, send, recv, k):
        return pltpu.make_async_remote_copy(
            src_ref=ref.at[col], dst_ref=ref.at[col], send_sem=send.at[k], recv_sem=recv.at[k],
            device_id=(row, col ^ k), device_id_type=MESH,
        )

    for k in range(1, ROWS):
        over_row(ybuf, y_send, y_recv, k).start()
    for k in range(1, COLS):
        over_col(xbuf, x_send, x_recv, k).start()

    lane = lax.broadcasted_iota(jnp.int32, (LANES, LANES), 1)
    line = lax.broadcasted_iota(jnp.int32, (LANES, LANES), 0)
    eye = lane == line
    lower = lane < LATENT
    lane8 = lax.broadcasted_iota(jnp.int32, (8, LANES), 1)
    line8 = lax.broadcasted_iota(jnp.int32, (8, LANES), 0)

    def build_right(k, carry):
        @pl.when(k > 0)
        def _():
            over_row(ybuf, y_send, y_recv, k).wait_recv()
        peer = row ^ k
        high, mid, low = pieces(ybuf[peer, 0:LATENT, :])
        at = pl.ds(pl.multiple_of(peer * LANES, LANES), LANES)
        for place, piece in enumerate((high, mid, high, mid, low, high)):
            right[LATENT * place : LATENT * (place + 1), at] = piece
        return carry

    lax.fori_loop(0, ROWS, build_right, 0)

    def set_vbias(pot):
        for a in range(2):
            for c in range(GROUPS):
                vbias[a, c, :, :] = jnp.broadcast_to(pot[c] + bias(a, c // 8), (8, LANES))

    set_vbias([-ybuf[c, LATENT + 1 : LATENT + 2, :] for c in range(GROUPS)])

    def row_block(g, pot):
        def one(k, carry):
            acc_peak, acc_total = carry
            at = pl.ds(pl.multiple_of(g * LANES + 8 * k, 8), 8)
            t = [score[c, at, :] + pot[c] for c in range(GROUPS)]
            peak = tree(jnp.maximum, t)
            total = tree(jnp.add, [jnp.exp2(v - peak) for v in t])
            top = jnp.max(peak, axis=1, keepdims=True)
            whole = jnp.sum(total * jnp.exp2(peak - top), axis=1, keepdims=True)
            here = lane8 == line8 + 8 * k
            return (
                acc_peak + jnp.where(here, top, 0.0),
                acc_total + jnp.where(here, whole, 0.0),
            )

        zero = jnp.zeros((8, LANES), jnp.float32)
        acc_peak, acc_total = lax.fori_loop(0, 16, one, (zero, zero), unroll=4)
        peak_rows[pl.ds(g, 1), :] = jnp.sum(acc_peak, axis=0, keepdims=True)
        total_rows[pl.ds(g, 1), :] = jnp.sum(acc_total, axis=0, keepdims=True)

    def first_rows(k, carry):
        @pl.when(k > 0)
        def _():
            over_col(xbuf, x_send, x_recv, k).wait_recv()
        peer = col ^ k
        packed = xbuf[peer, 0:LANES, :]
        turned = pltpu.roll(packed, LATENT, 1)
        for half in range(2):
            if half == 0:
                twice = jnp.where(lower, packed, turned)
            else:
                twice = jnp.where(lower, turned, packed)
            high, mid, low = pieces(twice)
            at = slice(half * LANES, (half + 1) * LANES)
            left[at, 0:LANES] = high
            left[at, LANES : 2 * LANES] = mid
            left[at, 2 * LANES : 3 * LANES] = jnp.where(lower, twice, low.astype(jnp.float32)).astype(jnp.bfloat16)
        at = pl.ds(pl.multiple_of(peer * 256, 256), 256)
        for n in range(4):
            res = jnp.dot(left[...], right[:, n * 512 : (n + 1) * 512], preferred_element_type=jnp.float32)
            for c in range(4):
                score[n * 4 + c, at, :] = res[:, c * LANES : (c + 1) * LANES]
        pot = [vbias[peer // 4, c] for c in range(GROUPS)]
        row_block(2 * peer, pot)
        row_block(2 * peer + 1, pot)
        return carry

    lax.fori_loop(0, COLS, first_rows, 0)

    def exchange_u(step):
        upart[step, col] = peak_rows[...] + jnp.log2(total_rows[...])
        for k in range(1, COLS):
            over_col(upart.at[step], u_send.at[step], u_recv.at[step], k).start()
        for k in range(1, COLS):
            over_col(upart.at[step], u_send.at[step], u_recv.at[step], k).wait_recv()
        parts = [upart[step, k] for k in range(COLS)]
        top = tree(jnp.maximum, parts)
        total = tree(jnp.add, [jnp.exp2(p - top) for p in parts])
        mass = jnp.concatenate([xbuf[k, LANES : LANES + 2, :] for k in range(COLS)], axis=0)
        pot = mass - (top + jnp.log2(total))
        for k in range(GROUPS):
            spread = jnp.where(eye, jnp.broadcast_to(pot[k : k + 1, :], (LANES, LANES)), 0.0)
            wide = jnp.sum(spread, axis=1, keepdims=True)
            ucol[k * LANES : (k + 1) * LANES, :] = jnp.broadcast_to(wide, (LANES, LANES))
        return pot

    def exchange_v(step):
        vpart[step, row] = peak_rows[...] + jnp.log2(total_rows[...])
        for k in range(1, ROWS):
            over_row(vpart.at[step], v_send.at[step], v_recv.at[step], k).start()
        for k in range(1, ROWS):
            over_row(vpart.at[step], v_send.at[step], v_recv.at[step], k).wait_recv()
        parts = [vpart[step, k] for k in range(ROWS)]
        top = tree(jnp.maximum, parts)
        total = tree(jnp.add, [jnp.exp2(p - top) for p in parts])
        mass = jnp.concatenate([ybuf[k, LATENT : LATENT + 1, :] for k in range(ROWS)], axis=0)
        return mass - (top + jnp.log2(total))

    def column_pass():
        def chunk(c, carry):
            live = [bias(0, c // 8), bias(1, c // 8)]
            peaks, totals = [], []
            for g in range(GROUPS):
                t = [
                    score[c, g * LANES + 8 * k : g * LANES + 8 * k + 8, :]
                    + ucol[g * LANES + 8 * k : g * LANES + 8 * k + 8, :]
                    for k in range(16)
                ]
                peak = tree(jnp.maximum, t)
                totals.append(tree(jnp.add, [jnp.exp2(v - peak) for v in t]))
                peaks.append(peak + live[g // 8])
            top = tree(jnp.maximum, peaks)
            total = tree(jnp.add, [q * jnp.exp2(p - top) for p, q in zip(peaks, totals)])
            whole_top = jnp.max(top, axis=0, keepdims=True)
            peak_rows[pl.ds(c, 1), :] = whole_top
            total_rows[pl.ds(c, 1), :] = jnp.sum(total * jnp.exp2(top - whole_top), axis=0, keepdims=True)
            return carry

        lax.fori_loop(0, GROUPS, chunk, 0)

    def row_pass():
        def block(g, carry):
            pot = [vbias[g // 8, c] for c in range(GROUPS)]
            row_block(g, pot)
            return carry

        lax.fori_loop(0, GROUPS, block, 0)

    exchange_u(0)
    column_pass()
    pot = exchange_v(0)
    set_vbias([pot[c : c + 1, :] for c in range(GROUPS)])
    row_pass()
    upot = exchange_u(1)
    x_halves = jnp.concatenate([xbuf[k, LANES + 2 : LANES + 4, :] for k in range(COLS)], axis=0)
    u_ref[...] = BACK * (upot + x_halves)
    column_pass()
    vpot = exchange_v(1)
    y_halves = jnp.concatenate([ybuf[k, LATENT + 1 : LATENT + 2, :] for k in range(ROWS)], axis=0)
    v_ref[...] = BACK * (vpot + y_halves)

    for k in range(1, ROWS):
        over_row(ybuf, y_send, y_recv, k).wait_send()
        for step in range(2):
            over_row(vpart.at[step], v_send.at[step], v_recv.at[step], k).wait_send()
    for k in range(1, COLS):
        over_col(xbuf, x_send, x_recv, k).wait_send()
        for step in range(2):
            over_col(upart.at[step], u_send.at[step], u_recv.at[step], k).wait_send()


def local(source_cells, target_cells, source_mass, target_mass, support):
    vmem = pl.BlockSpec(memory_space=pltpu.VMEM)
    u, v = pl.pallas_call(
        kernel,
        out_shape=(
            jax.ShapeDtypeStruct((GROUPS, LANES), jnp.float32),
            jax.ShapeDtypeStruct((GROUPS, LANES), jnp.float32),
        ),
        in_specs=[vmem, vmem, vmem, vmem, pl.BlockSpec(memory_space=pltpu.SMEM)],
        out_specs=(vmem, vmem),
        scratch_shapes=[
            pltpu.VMEM((COLS, LANES + 8, LANES), jnp.float32),
            pltpu.VMEM((ROWS, LATENT + 8, LANES), jnp.float32),
            pltpu.VMEM((256, 384), jnp.bfloat16),
            pltpu.VMEM((384, 2048), jnp.bfloat16),
            pltpu.VMEM((GROUPS, 2048, LANES), jnp.float32),
            pltpu.VMEM((2, COLS, GROUPS, LANES), jnp.float32),
            pltpu.VMEM((2, ROWS, GROUPS, LANES), jnp.float32),
            pltpu.VMEM((2048, LANES), jnp.float32),
            pltpu.VMEM((2, GROUPS, 8, LANES), jnp.float32),
            pltpu.VMEM((GROUPS, LANES), jnp.float32),
            pltpu.VMEM((GROUPS, LANES), jnp.float32),
            pltpu.SemaphoreType.DMA((COLS,)),
            pltpu.SemaphoreType.DMA((COLS,)),
            pltpu.SemaphoreType.DMA((ROWS,)),
            pltpu.SemaphoreType.DMA((ROWS,)),
            pltpu.SemaphoreType.DMA((2, COLS)),
            pltpu.SemaphoreType.DMA((2, COLS)),
            pltpu.SemaphoreType.DMA((2, ROWS)),
            pltpu.SemaphoreType.DMA((2, ROWS)),
        ],
        compiler_params=pltpu.CompilerParams(
            collective_id=0, has_side_effects=True, vmem_limit_bytes=48 * 1024 * 1024
        ),
        name="sinkhorn",
    )(
        source_cells,
        target_cells,
        source_mass.reshape(2, LANES),
        target_mass.reshape(1, LANES),
        support,
    )
    return u.reshape(2048), v.reshape(2048)


def solution(mesh):
    return jax.shard_map(
        local,
        mesh=mesh,
        in_specs=(
            P(("row", "col"), None),
            P(("col", "row"), None),
            P(("row", "col")),
            P(("col", "row")),
            P("row", "col"),
        ),
        out_specs=(P("row"), P("col")),
        check_vma=False,
    )
```

```python
import math

import jax
import jax.numpy as jnp
from jax import lax
from jax.experimental import pallas as pl
from jax.experimental.pallas import tpu as pltpu
from jax.sharding import PartitionSpec as P

MESH = pl.DeviceIdType.MESH
LATENT = 64
ROWS = 16
COLS = 8
LANES = 128
GROUPS = 16
TERMS = 384
EPSILON = 0.02
NEGATIVE = -1e30
SCALE = math.sqrt(2.0 * math.log2(math.e) / (LATENT * EPSILON))
BACK = EPSILON * math.log(2.0)
FAR_FIRST = tuple(sorted(range(1, ROWS), key=lambda k: -((0, 1, 2, 1)[k & 3] + (0, 1, 2, 1)[k >> 2])))


def pieces(value):
    high = value.astype(jnp.bfloat16)
    rest = value - high.astype(jnp.float32)
    mid = rest.astype(jnp.bfloat16)
    low = (rest - mid.astype(jnp.float32)).astype(jnp.bfloat16)
    return high, mid, low


def tree(op, parts):
    parts = list(parts)
    while len(parts) > 1:
        parts = [
            op(parts[k], parts[k + 1]) if k + 1 < len(parts) else parts[k]
            for k in range(0, len(parts), 2)
        ]
    return parts[0]


def gray(i):
    return i ^ (i // 2)


def kernel(
    x_hbm, y_hbm, a_hbm, b_hbm, support_hbm, u_ref, v_ref,
    x_ref, y_ref, a_ref, b_ref, support_ref,
    xbuf, ybuf, left, right, score, upart, vpart, ucol, vbias,
    row_peak, row_total, col_peak, col_total,
    in_sem, x_send, x_recv, relay_send, relay_recv, y_send, y_recv, u_send, u_recv, v_send, v_recv,
):
    row = lax.axis_index("row")
    col = lax.axis_index("col")
    my_z = row // 4
    my_x = col // 2

    loads = [
        pltpu.make_async_copy(src, dst, in_sem.at[k])
        for k, (src, dst) in enumerate(
            ((x_hbm, x_ref), (y_hbm, y_ref), (a_hbm, a_ref), (b_hbm, b_ref), (support_hbm, support_ref))
        )
    ]
    for load in loads:
        load.start()

    barrier = pltpu.get_barrier_semaphore()
    for k in FAR_FIRST:
        pl.semaphore_signal(barrier, inc=1, device_id=(row ^ k, col), device_id_type=MESH)
    for k in range(1, COLS):
        pl.semaphore_signal(barrier, inc=1, device_id=(row, col ^ k), device_id_type=MESH)

    def bias(a, b):
        return jnp.where(support_ref[a, b] == 1, jnp.float32(0.0), jnp.float32(NEGATIVE))

    def over_row(ref, send, recv, k):
        return pltpu.make_async_remote_copy(
            src_ref=ref.at[row], dst_ref=ref.at[row], send_sem=send.at[k], recv_sem=recv.at[k],
            device_id=(row ^ k, col), device_id_type=MESH,
        )

    def over_col(ref, send, recv, k):
        return pltpu.make_async_remote_copy(
            src_ref=ref.at[col], dst_ref=ref.at[col], send_sem=send.at[k], recv_sem=recv.at[k],
            device_id=(row, col ^ k), device_id_type=MESH,
        )

    def relay(owner, k):
        return pltpu.make_async_remote_copy(
            src_ref=xbuf.at[owner], dst_ref=xbuf.at[owner], send_sem=relay_send.at[k], recv_sem=relay_recv.at[k],
            device_id=(row, col ^ 1), device_id_type=MESH,
        )

    for load in loads:
        load.wait()
    x_cells = x_ref[...] * SCALE
    x_half = 0.5 * jnp.sum(x_cells * x_cells, axis=0, keepdims=True)
    both = jnp.concatenate([x_cells[:, 0:LANES], x_cells[:, LANES : 2 * LANES]], axis=0)
    xbuf[col, 0:LANES, :] = both.T
    xbuf[col, LANES : LANES + 8, :] = jnp.concatenate(
        [jnp.log2(a_ref[...]), x_half[:, 0:LANES], x_half[:, LANES : 2 * LANES], jnp.zeros((4, LANES), jnp.float32)],
        axis=0,
    )
    y_cells = y_ref[...] * SCALE
    ybuf[row, 0:LATENT, :] = y_cells
    ybuf[row, LATENT : LATENT + 8, :] = jnp.concatenate(
        [
            jnp.log2(b_ref[...]),
            0.5 * jnp.sum(y_cells * y_cells, axis=0, keepdims=True),
            jnp.zeros((6, LANES), jnp.float32),
        ],
        axis=0,
    )

    def clear(i, carry):
        at = pl.ds(pl.multiple_of(i * LANES, LANES), LANES)
        row_peak[at, :] = jnp.full((LANES, LANES), 3.0 * NEGATIVE, jnp.float32)
        row_total[at, :] = jnp.zeros((LANES, LANES), jnp.float32)
        return carry

    lax.fori_loop(0, GROUPS, clear, 0)

    pl.semaphore_wait(barrier, COLS + ROWS - 2)

    for k in (4, 2, 6, 1):
        over_col(xbuf, x_send, x_recv, k).start()
    for k in FAR_FIRST:
        over_row(ybuf, y_send, y_recv, k).start()

    lower = lax.broadcasted_iota(jnp.int32, (LANES, LANES), 1) < LATENT
    eye = lax.broadcasted_iota(jnp.int32, (LANES, LANES), 0) == lax.broadcasted_iota(jnp.int32, (LANES, LANES), 1)

    def build_right(level):
        zg = my_z ^ gray(level)
        for yy in range(4):
            k = 4 * gray(level) + yy
            if k > 0:
                over_row(ybuf, y_send, y_recv, k).wait_recv()
        for yy in range(4):
            high, mid, low = pieces(ybuf[zg * 4 + yy, 0:LATENT, :])
            at = slice(yy * LANES, (yy + 1) * LANES)
            for place, piece in enumerate((high, mid, high, mid, low, high)):
                right[zg, LATENT * place : LATENT * (place + 1), at] = piece
            start = -ybuf[zg * 4 + yy, LATENT + 1 : LATENT + 2, :]
            for a in range(2):
                vbias[a, zg * 4 + yy] = jnp.broadcast_to(start + bias(a, zg // 2), (8, LANES))

    def build_left(level):
        xg = my_x ^ gray(level)
        for e in range(2):
            packed = xbuf[2 * xg + e, 0:LANES, :]
            turned = pltpu.roll(packed, LATENT, 1)
            for half in range(2):
                if half == 0:
                    twice = jnp.where(lower, packed, turned)
                else:
                    twice = jnp.where(lower, turned, packed)
                high, mid, low = pieces(twice)
                at = slice((2 * e + half) * LANES, (2 * e + half + 1) * LANES)
                left[xg, at, 0:LANES] = high
                left[xg, at, LANES : 2 * LANES] = mid
                left[xg, at, 2 * LANES : 3 * LANES] = jnp.where(
                    lower, high.astype(jnp.float32), low.astype(jnp.float32)
                ).astype(jnp.bfloat16)

    def tile(xg, zg):
        pot = [vbias[xg // 2, zg * 4 + c] for c in range(4)]
        base = xg * 512
        for i in range(4):
            res = jnp.dot(
                left[xg, i * LANES : (i + 1) * LANES, :], right[zg], preferred_element_type=jnp.float32
            )
            for c in range(4):
                at = pl.ds(pl.multiple_of(base + i * LANES, LANES), LANES)
                score[zg * 4 + c, at, :] = res[:, c * LANES : (c + 1) * LANES]
            for q in range(GROUPS):
                at = pl.ds(pl.multiple_of(base + i * LANES + 8 * q, 8), 8)
                t = [res[8 * q : 8 * q + 8, c * LANES : (c + 1) * LANES] + pot[c] for c in range(4)]
                old = row_peak[at, :]
                new = jnp.maximum(tree(jnp.maximum, t), old)
                total = tree(jnp.add, [jnp.exp2(value - new) for value in t])
                row_total[at, :] = row_total[at, :] * jnp.exp2(old - new) + total
                row_peak[at, :] = new

    def finish_rows(step, xg, block, peak, total):
        peak, total = peak.T, total.T
        top = jnp.max(peak, axis=0, keepdims=True)
        whole = jnp.sum(total * jnp.exp2(peak - top), axis=0, keepdims=True)
        upart[step, xg, col, pl.ds(block, 1), :] = top + jnp.log2(whole)

    def send_u(step, xg):
        for k in range(1, COLS):
            over_col(upart.at[step, xg], u_send.at[step, xg], u_recv.at[step, xg], k).start()

    for k in (2, 6):
        over_col(xbuf, x_send, x_recv, k).wait_recv()
        relay(col ^ k, k).start()
    over_col(xbuf, x_send, x_recv, 1).wait_recv()
    build_left(0)
    build_right(0)
    tile(my_x, my_z)
    over_col(xbuf, x_send, x_recv, 4).wait_recv()
    relay(col ^ 4, 4).start()
    build_right(1)
    relay(col ^ 3, 2).wait_recv()
    build_left(1)

    def several(count, xs, zs):
        def body(i, carry):
            tile(xs(i), zs(i))
            return carry

        lax.fori_loop(0, count, body, 0)

    several(3, lambda i: my_x ^ gray((i + 1) // 2), lambda i: my_z ^ gray(1 - i % 2))
    build_right(2)
    relay(col ^ 7, 6).wait_recv()
    build_left(2)
    several(5, lambda i: my_x ^ gray(jnp.minimum(i, 2)), lambda i: my_z ^ gray(jnp.where(i < 2, 2, i - 2)))
    relay(col ^ 5, 4).wait_recv()
    build_left(3)
    several(3, lambda i: my_x ^ gray(3), lambda i: my_z ^ gray(i))
    build_right(3)

    def last(xg, carry):
        tile(xg, my_z ^ gray(3))
        for block in range(4):
            at = pl.ds(pl.multiple_of(xg * 512 + block * LANES, LANES), LANES)
            finish_rows(0, xg, block, row_peak[at, :], row_total[at, :])
        send_u(0, xg)
        return carry

    lax.fori_loop(0, 4, last, 0)

    def combine_u(step, xg):
        for k in range(1, COLS):
            over_col(upart.at[step, xg], u_send.at[step, xg], u_recv.at[step, xg], k).wait_recv()
        parts = [upart[step, xg, k] for k in range(COLS)]
        top = tree(jnp.maximum, parts)
        total = tree(jnp.add, [jnp.exp2(p - top) for p in parts])
        mass = jnp.concatenate([xbuf[2 * xg + e, LANES : LANES + 2, :] for e in range(2)], axis=0)
        pot = mass - (top + jnp.log2(total))
        for block in range(4):
            spread = jnp.where(eye, jnp.broadcast_to(pot[block : block + 1, :], (LANES, LANES)), 0.0)
            wide = jnp.sum(spread, axis=1, keepdims=True)
            ucol[block * LANES : (block + 1) * LANES, :] = jnp.broadcast_to(wide, (LANES, LANES))
        if step == 1:
            half = jnp.concatenate([xbuf[2 * xg + e, LANES + 2 : LANES + 4, :] for e in range(2)], axis=0)
            u_ref[pl.ds(xg * 4, 4), :] = BACK * (pot + half)

    def column_pass(step):
        col_peak[...] = jnp.full((GROUPS, 8, LANES), 3.0 * NEGATIVE, jnp.float32)
        col_total[...] = jnp.zeros((GROUPS, 8, LANES), jnp.float32)

        def body(t, carry):
            xg, quad = t // 4, t % 4

            @pl.when(quad == 0)
            def _():
                combine_u(step, xg)

            live = bias(xg // 2, quad // 2)
            base = xg * 512
            peaks = [[col_peak[4 * quad + c]] for c in range(4)]
            totals = [[col_total[4 * quad + c]] for c in range(4)]
            for g in range(4):
                pots = [ucol[g * LANES + 8 * k : g * LANES + 8 * k + 8, :] for k in range(GROUPS)]
                for c in range(4):
                    values = [
                        score[4 * quad + c, pl.ds(pl.multiple_of(base + g * LANES + 8 * k, 8), 8), :] + pots[k]
                        for k in range(GROUPS)
                    ]
                    peak = tree(jnp.maximum, values)
                    totals[c].append(tree(jnp.add, [jnp.exp2(value - peak) for value in values]))
                    peaks[c].append(peak + live)
            for c in range(4):
                top = tree(jnp.maximum, peaks[c])
                total = tree(jnp.add, [q * jnp.exp2(p - top) for p, q in zip(peaks[c], totals[c])])
                col_peak[4 * quad + c] = top
                col_total[4 * quad + c] = total

            @pl.when(xg == 3)
            def _():
                lines = []
                for c in range(4):
                    peak, total = col_peak[4 * quad + c], col_total[4 * quad + c]
                    top = jnp.max(peak, axis=0, keepdims=True)
                    whole = jnp.sum(total * jnp.exp2(peak - top), axis=0, keepdims=True)
                    lines.append(top + jnp.log2(whole))
                vpart[step, quad // 2, row, pl.ds(quad % 2 * 4, 4), :] = jnp.concatenate(lines, axis=0)

            @pl.when(jnp.logical_and(xg == 3, quad % 2 == 1))
            def _():
                half = quad // 2
                for k in FAR_FIRST:
                    over_row(vpart.at[step, half], v_send.at[step, half], v_recv.at[step, half], k).start()

            return carry

        lax.fori_loop(0, GROUPS, body, 0)

    def combine_v(step, half):
        for k in FAR_FIRST[::-1]:
            over_row(vpart.at[step, half], v_send.at[step, half], v_recv.at[step, half], k).wait_recv()
        parts = [vpart[step, half, k] for k in range(ROWS)]
        top = tree(jnp.maximum, parts)
        total = tree(jnp.add, [jnp.exp2(p - top) for p in parts])
        mass = jnp.concatenate([ybuf[8 * half + k, LATENT : LATENT + 1, :] for k in range(8)], axis=0)
        return mass - (top + jnp.log2(total))

    column_pass(0)
    for half in range(2):
        pot = combine_v(0, half)
        for a in range(2):
            shifted = pot + bias(a, half)
            for c in range(8):
                vbias[a, 8 * half + c] = jnp.broadcast_to(shifted[c : c + 1, :], (8, LANES))

    def row_block(t, carry):
        xg, block = t // 4, t % 4
        pot = [vbias[xg // 2, c] for c in range(GROUPS)]
        peaks, totals = [], []
        for k in range(GROUPS):
            at = pl.ds(pl.multiple_of(t * LANES + 8 * k, 8), 8)
            values = [score[c, at, :] + pot[c] for c in range(GROUPS)]
            peak = tree(jnp.maximum, values)
            totals.append(tree(jnp.add, [jnp.exp2(value - peak) for value in values]))
            peaks.append(peak)
        finish_rows(1, xg, block, jnp.concatenate(peaks, axis=0), jnp.concatenate(totals, axis=0))

        @pl.when(block == 3)
        def _():
            send_u(1, xg)

        return carry

    lax.fori_loop(0, GROUPS, row_block, 0)
    column_pass(1)
    for half in range(2):
        pot = combine_v(1, half)
        y_half = jnp.concatenate([ybuf[8 * half + k, LATENT + 1 : LATENT + 2, :] for k in range(8)], axis=0)
        v_ref[8 * half : 8 * half + 8, :] = BACK * (pot + y_half)

    for k in FAR_FIRST:
        over_row(ybuf, y_send, y_recv, k).wait_send()
        for step in range(2):
            for half in range(2):
                over_row(vpart.at[step, half], v_send.at[step, half], v_recv.at[step, half], k).wait_send()
    for k in (4, 2, 6, 1):
        over_col(xbuf, x_send, x_recv, k).wait_send()
    for k in (2, 6, 4):
        relay(col ^ k, k).wait_send()
    for k in range(1, COLS):
        for step in range(2):
            for xg in range(4):
                over_col(upart.at[step, xg], u_send.at[step, xg], u_recv.at[step, xg], k).wait_send()


def local(source_cells, target_cells, source_mass, target_mass, support):
    vmem = pl.BlockSpec(memory_space=pltpu.VMEM)
    hbm = pl.BlockSpec(memory_space=pl.ANY)
    u, v = pl.pallas_call(
        kernel,
        out_shape=(
            jax.ShapeDtypeStruct((GROUPS, LANES), jnp.float32),
            jax.ShapeDtypeStruct((GROUPS, LANES), jnp.float32),
        ),
        in_specs=[hbm] * 5,
        out_specs=(vmem, vmem),
        scratch_shapes=[
            pltpu.VMEM((LATENT, 256), jnp.float32),
            pltpu.VMEM((LATENT, LANES), jnp.float32),
            pltpu.VMEM((2, LANES), jnp.float32),
            pltpu.VMEM((1, LANES), jnp.float32),
            pltpu.SMEM((2, 2), jnp.int32),
            pltpu.VMEM((COLS, LANES + 8, LANES), jnp.float32),
            pltpu.VMEM((ROWS, LATENT + 8, LANES), jnp.float32),
            pltpu.VMEM((4, 512, TERMS), jnp.bfloat16),
            pltpu.VMEM((4, TERMS, 512), jnp.bfloat16),
            pltpu.VMEM((GROUPS, 2048, LANES), jnp.float32),
            pltpu.VMEM((2, 4, COLS, 4, LANES), jnp.float32),
            pltpu.VMEM((2, 2, ROWS, 8, LANES), jnp.float32),
            pltpu.VMEM((512, LANES), jnp.float32),
            pltpu.VMEM((2, GROUPS, 8, LANES), jnp.float32),
            pltpu.VMEM((2048, LANES), jnp.float32),
            pltpu.VMEM((2048, LANES), jnp.float32),
            pltpu.VMEM((GROUPS, 8, LANES), jnp.float32),
            pltpu.VMEM((GROUPS, 8, LANES), jnp.float32),
            pltpu.SemaphoreType.DMA((5,)),
            pltpu.SemaphoreType.DMA((COLS,)),
            pltpu.SemaphoreType.DMA((COLS,)),
            pltpu.SemaphoreType.DMA((COLS,)),
            pltpu.SemaphoreType.DMA((COLS,)),
            pltpu.SemaphoreType.DMA((ROWS,)),
            pltpu.SemaphoreType.DMA((ROWS,)),
            pltpu.SemaphoreType.DMA((2, 4, COLS)),
            pltpu.SemaphoreType.DMA((2, 4, COLS)),
            pltpu.SemaphoreType.DMA((2, 2, ROWS)),
            pltpu.SemaphoreType.DMA((2, 2, ROWS)),
        ],
        compiler_params=pltpu.CompilerParams(
            collective_id=0, has_side_effects=True, vmem_limit_bytes=48 * 1024 * 1024
        ),
        name="sinkhorn",
    )(
        source_cells.T,
        target_cells.T,
        source_mass.reshape(2, LANES),
        target_mass.reshape(1, LANES),
        support,
    )
    return u.reshape(2048), v.reshape(2048)


def solution(mesh):
    return jax.shard_map(
        local,
        mesh=mesh,
        in_specs=(
            P(("row", "col"), None),
            P(("col", "row"), None),
            P(("row", "col")),
            P(("col", "row")),
            P("row", "col"),
        ),
        out_specs=(P("row"), P("col")),
        check_vma=False,
    )
```

```python
import math

import jax
import jax.numpy as jnp
from jax import lax
from jax.experimental import pallas as pl
from jax.experimental.pallas import tpu as pltpu
from jax.sharding import PartitionSpec as P

MESH = pl.DeviceIdType.MESH
LATENT = 64
ROWS = 16
COLS = 8
LANES = 128
GROUPS = 16
TERMS = 384
EPSILON = 0.02
NEGATIVE = -1e30
SCALE = math.sqrt(2.0 * math.log2(math.e) / (LATENT * EPSILON))
BACK = EPSILON * math.log(2.0)
FAR_FIRST = tuple(sorted(range(1, ROWS), key=lambda k: -((0, 1, 2, 1)[k & 3] + (0, 1, 2, 1)[k >> 2])))


def pieces(value):
    high = value.astype(jnp.bfloat16)
    rest = value - high.astype(jnp.float32)
    mid = rest.astype(jnp.bfloat16)
    low = (rest - mid.astype(jnp.float32)).astype(jnp.bfloat16)
    return high, mid, low


def tree(op, parts):
    parts = list(parts)
    while len(parts) > 1:
        parts = [
            op(parts[k], parts[k + 1]) if k + 1 < len(parts) else parts[k]
            for k in range(0, len(parts), 2)
        ]
    return parts[0]


def gray(i):
    return i ^ (i // 2)


def kernel(
    x_hbm, y_hbm, a_hbm, b_hbm, support_hbm, u_ref, v_ref,
    x_ref, y_ref, a_ref, b_ref, support_ref,
    xbuf, ybuf, left, right, score, upart, vpart, ucol, vbias,
    row_peak, row_total, col_peak, col_total,
    in_sem, sent, x_recv, relay_recv, y_recv, u_recv, v_recv,
):
    row = lax.axis_index("row")
    col = lax.axis_index("col")
    my_z = row // 4
    my_x = col // 2

    loads = [
        pltpu.make_async_copy(src, dst, in_sem.at[k])
        for k, (src, dst) in enumerate(
            ((x_hbm, x_ref), (y_hbm, y_ref), (a_hbm, a_ref), (b_hbm, b_ref), (support_hbm, support_ref))
        )
    ]
    for load in loads:
        load.start()

    barrier = pltpu.get_barrier_semaphore()
    for k in FAR_FIRST:
        pl.semaphore_signal(barrier, inc=1, device_id=(row ^ k, col), device_id_type=MESH)
    for k in range(1, COLS):
        pl.semaphore_signal(barrier, inc=1, device_id=(row, col ^ k), device_id_type=MESH)

    def bias(a, b):
        return jnp.where(support_ref[a, b] == 1, jnp.float32(0.0), jnp.float32(NEGATIVE))

    def over_row(ref, send, recv, k):
        return pltpu.make_async_remote_copy(
            src_ref=ref.at[row], dst_ref=ref.at[row], send_sem=send, recv_sem=recv,
            device_id=(row ^ k, col), device_id_type=MESH,
        )

    def over_col(ref, send, recv, k):
        return pltpu.make_async_remote_copy(
            src_ref=ref.at[col], dst_ref=ref.at[col], send_sem=send, recv_sem=recv,
            device_id=(row, col ^ k), device_id_type=MESH,
        )

    def relay(owner, k):
        return pltpu.make_async_remote_copy(
            src_ref=xbuf.at[owner], dst_ref=xbuf.at[owner], send_sem=sent.at[1], recv_sem=relay_recv.at[k // 2],
            device_id=(row, col ^ 1), device_id_type=MESH,
        )

    def all_of(ref, sem):
        return pltpu.make_async_copy(ref, ref, sem)

    for load in loads:
        load.wait()
    x_cells = x_ref[...] * SCALE
    x_half = 0.5 * jnp.sum(x_cells * x_cells, axis=0, keepdims=True)
    both = jnp.concatenate([x_cells[:, 0:LANES], x_cells[:, LANES : 2 * LANES]], axis=0)
    xbuf[col, 0:LANES, :] = both.T
    xbuf[col, LANES : LANES + 8, :] = jnp.concatenate(
        [jnp.log2(a_ref[...]), x_half[:, 0:LANES], x_half[:, LANES : 2 * LANES], jnp.zeros((4, LANES), jnp.float32)],
        axis=0,
    )
    y_cells = y_ref[...] * SCALE
    ybuf[row, 0:LATENT, :] = y_cells
    ybuf[row, LATENT : LATENT + 8, :] = jnp.concatenate(
        [
            jnp.log2(b_ref[...]),
            0.5 * jnp.sum(y_cells * y_cells, axis=0, keepdims=True),
            jnp.zeros((6, LANES), jnp.float32),
        ],
        axis=0,
    )

    def clear(i, carry):
        at = pl.ds(pl.multiple_of(i * LANES, LANES), LANES)
        row_peak[at, :] = jnp.full((LANES, LANES), 3.0 * NEGATIVE, jnp.float32)
        row_total[at, :] = jnp.zeros((LANES, LANES), jnp.float32)
        return carry

    lax.fori_loop(0, GROUPS, clear, 0)

    pl.semaphore_wait(barrier, COLS + ROWS - 2)

    for k in (4, 2, 6, 1):
        over_col(xbuf, sent.at[0], x_recv.at[k // 2], k).start()
    for k in FAR_FIRST:
        over_row(ybuf, sent.at[2], y_recv.at[k // 4], k).start()

    lower = lax.broadcasted_iota(jnp.int32, (LANES, LANES), 1) < LATENT
    eye = lax.broadcasted_iota(jnp.int32, (LANES, LANES), 0) == lax.broadcasted_iota(jnp.int32, (LANES, LANES), 1)

    def build_right(level):
        zg = my_z ^ gray(level)
        count = 3 if level == 0 else 4
        all_of(ybuf.at[0:count], y_recv.at[gray(level)]).wait()
        for yy in range(4):
            high, mid, low = pieces(ybuf[zg * 4 + yy, 0:LATENT, :])
            at = slice(yy * LANES, (yy + 1) * LANES)
            for place, piece in enumerate((high, mid, high, mid, low, high)):
                right[zg, LATENT * place : LATENT * (place + 1), at] = piece
            start = -ybuf[zg * 4 + yy, LATENT + 1 : LATENT + 2, :]
            for a in range(2):
                vbias[a, zg * 4 + yy] = jnp.broadcast_to(start + bias(a, zg // 2), (8, LANES))

    def build_left(level):
        xg = my_x ^ gray(level)
        for e in range(2):
            packed = xbuf[2 * xg + e, 0:LANES, :]
            turned = pltpu.roll(packed, LATENT, 1)
            for half in range(2):
                if half == 0:
                    twice = jnp.where(lower, packed, turned)
                else:
                    twice = jnp.where(lower, turned, packed)
                high, mid, low = pieces(twice)
                at = slice((2 * e + half) * LANES, (2 * e + half + 1) * LANES)
                left[xg, at, 0:LANES] = high
                left[xg, at, LANES : 2 * LANES] = mid
                left[xg, at, 2 * LANES : 3 * LANES] = jnp.where(
                    lower, high.astype(jnp.float32), low.astype(jnp.float32)
                ).astype(jnp.bfloat16)

    def tile(xg, zg):
        pot = [vbias[xg // 2, zg * 4 + c] for c in range(4)]
        base = xg * 512
        for i in range(4):
            res = jnp.dot(
                left[xg, i * LANES : (i + 1) * LANES, :], right[zg], preferred_element_type=jnp.float32
            )
            for c in range(4):
                at = pl.ds(pl.multiple_of(base + i * LANES, LANES), LANES)
                score[zg * 4 + c, at, :] = res[:, c * LANES : (c + 1) * LANES]
            for q in range(GROUPS):
                at = pl.ds(pl.multiple_of(base + i * LANES + 8 * q, 8), 8)
                t = [res[8 * q : 8 * q + 8, c * LANES : (c + 1) * LANES] + pot[c] for c in range(4)]
                old = row_peak[at, :]
                new = jnp.maximum(tree(jnp.maximum, t), old)
                total = tree(jnp.add, [jnp.exp2(value - new) for value in t])
                row_total[at, :] = row_total[at, :] * jnp.exp2(old - new) + total
                row_peak[at, :] = new

    def finish_rows(step, xg, block, peak, total):
        peak, total = peak.T, total.T
        top = jnp.max(peak, axis=0, keepdims=True)
        whole = jnp.sum(total * jnp.exp2(peak - top), axis=0, keepdims=True)
        upart[step, xg, col, pl.ds(block, 1), :] = top + jnp.log2(whole)

    def send_u(step, xg):
        for k in range(1, COLS):
            over_col(upart.at[step, xg], sent.at[3 + step], u_recv.at[step, xg], k).start()

    for k in (2, 6):
        over_col(xbuf, sent.at[0], x_recv.at[k // 2], k).wait_recv()
        relay(col ^ k, k).start()
    over_col(xbuf, sent.at[0], x_recv.at[0], 1).wait_recv()
    build_left(0)
    build_right(0)
    tile(my_x, my_z)
    over_col(xbuf, sent.at[0], x_recv.at[2], 4).wait_recv()
    relay(col ^ 4, 4).start()
    build_right(1)
    relay(col ^ 3, 2).wait_recv()
    build_left(1)

    def several(count, xs, zs):
        def body(i, carry):
            tile(xs(i), zs(i))
            return carry

        lax.fori_loop(0, count, body, 0)

    several(3, lambda i: my_x ^ gray((i + 1) // 2), lambda i: my_z ^ gray(1 - i % 2))
    build_right(2)
    relay(col ^ 7, 6).wait_recv()
    build_left(2)
    several(5, lambda i: my_x ^ gray(jnp.minimum(i, 2)), lambda i: my_z ^ gray(jnp.where(i < 2, 2, i - 2)))
    relay(col ^ 5, 4).wait_recv()
    build_left(3)
    several(3, lambda i: my_x ^ gray(3), lambda i: my_z ^ gray(i))
    build_right(3)

    def last(xg, carry):
        tile(xg, my_z ^ gray(3))
        for block in range(4):
            at = pl.ds(pl.multiple_of(xg * 512 + block * LANES, LANES), LANES)
            finish_rows(0, xg, block, row_peak[at, :], row_total[at, :])
        send_u(0, xg)
        return carry

    lax.fori_loop(0, 4, last, 0)

    def combine_u(step, xg):
        all_of(upart.at[step, xg, 0 : COLS - 1], u_recv.at[step, xg]).wait()
        parts = [upart[step, xg, k] for k in range(COLS)]
        top = tree(jnp.maximum, parts)
        total = tree(jnp.add, [jnp.exp2(p - top) for p in parts])
        mass = jnp.concatenate([xbuf[2 * xg + e, LANES : LANES + 2, :] for e in range(2)], axis=0)
        pot = mass - (top + jnp.log2(total))
        for block in range(4):
            spread = jnp.where(eye, jnp.broadcast_to(pot[block : block + 1, :], (LANES, LANES)), 0.0)
            wide = jnp.sum(spread, axis=1, keepdims=True)
            ucol[block * LANES : (block + 1) * LANES, :] = jnp.broadcast_to(wide, (LANES, LANES))
        if step == 1:
            half = jnp.concatenate([xbuf[2 * xg + e, LANES + 2 : LANES + 4, :] for e in range(2)], axis=0)
            u_ref[pl.ds(xg * 4, 4), :] = (pot + half)

    def column_pass(step):
        col_peak[...] = jnp.full((GROUPS, 8, LANES), 3.0 * NEGATIVE, jnp.float32)
        col_total[...] = jnp.zeros((GROUPS, 8, LANES), jnp.float32)

        def body(t, carry):
            xg, quad = t // 4, t % 4

            @pl.when(quad == 0)
            def _():
                combine_u(step, xg)

            live = bias(xg // 2, quad // 2)
            base = xg * 512
            peaks = [[col_peak[4 * quad + c]] for c in range(4)]
            totals = [[col_total[4 * quad + c]] for c in range(4)]
            for g in range(4):
                pots = [ucol[g * LANES + 8 * k : g * LANES + 8 * k + 8, :] for k in range(GROUPS)]
                for c in range(4):
                    values = [
                        score[4 * quad + c, pl.ds(pl.multiple_of(base + g * LANES + 8 * k, 8), 8), :] + pots[k]
                        for k in range(GROUPS)
                    ]
                    peak = tree(jnp.maximum, values)
                    totals[c].append(tree(jnp.add, [jnp.exp2(value - peak) for value in values]))
                    peaks[c].append(peak + live)
            for c in range(4):
                top = tree(jnp.maximum, peaks[c])
                total = tree(jnp.add, [q * jnp.exp2(p - top) for p, q in zip(peaks[c], totals[c])])
                col_peak[4 * quad + c] = top
                col_total[4 * quad + c] = total

            @pl.when(xg == 3)
            def _():
                lines = []
                for c in range(4):
                    peak, total = col_peak[4 * quad + c], col_total[4 * quad + c]
                    top = jnp.max(peak, axis=0, keepdims=True)
                    whole = jnp.sum(total * jnp.exp2(peak - top), axis=0, keepdims=True)
                    lines.append(top + jnp.log2(whole))
                vpart[step, quad // 2, row, pl.ds(quad % 2 * 4, 4), :] = jnp.concatenate(lines, axis=0)

            @pl.when(jnp.logical_and(xg == 3, quad % 2 == 1))
            def _():
                half = quad // 2
                for k in FAR_FIRST:
                    over_row(vpart.at[step, half], sent.at[5 + step], v_recv.at[step, half], k).start()

            return carry

        lax.fori_loop(0, GROUPS, body, 0)

    def combine_v(step, half):
        all_of(vpart.at[step, half, 0 : ROWS - 1], v_recv.at[step, half]).wait()
        parts = [vpart[step, half, k] for k in range(ROWS)]
        top = tree(jnp.maximum, parts)
        total = tree(jnp.add, [jnp.exp2(p - top) for p in parts])
        mass = jnp.concatenate([ybuf[8 * half + k, LATENT : LATENT + 1, :] for k in range(8)], axis=0)
        return mass - (top + jnp.log2(total))

    column_pass(0)
    for half in range(2):
        pot = combine_v(0, half)
        for a in range(2):
            shifted = pot + bias(a, half)
            for c in range(8):
                vbias[a, 8 * half + c] = jnp.broadcast_to(shifted[c : c + 1, :], (8, LANES))

    def row_block(t, carry):
        xg, block = t // 4, t % 4
        pot = [vbias[xg // 2, c] for c in range(GROUPS)]
        peaks, totals = [], []
        for k in range(GROUPS):
            at = pl.ds(pl.multiple_of(t * LANES + 8 * k, 8), 8)
            values = [score[c, at, :] + pot[c] for c in range(GROUPS)]
            peak = tree(jnp.maximum, values)
            totals.append(tree(jnp.add, [jnp.exp2(value - peak) for value in values]))
            peaks.append(peak)
        finish_rows(1, xg, block, jnp.concatenate(peaks, axis=0), jnp.concatenate(totals, axis=0))

        @pl.when(block == 3)
        def _():
            send_u(1, xg)

        return carry

    lax.fori_loop(0, GROUPS, row_block, 0)
    column_pass(1)
    all_of(xbuf.at[0:4], sent.at[0]).wait()
    all_of(xbuf.at[0:3], sent.at[1]).wait()
    all_of(ybuf.at[0 : ROWS - 1], sent.at[2]).wait()
    for step in range(2):
        all_of(upart.at[step, :, 0 : COLS - 1], sent.at[3 + step]).wait()
        all_of(vpart.at[step, :, 0 : ROWS - 1], sent.at[5 + step]).wait()
    for half in range(2):
        pot = combine_v(1, half)
        y_half = jnp.concatenate([ybuf[8 * half + k, LATENT + 1 : LATENT + 2, :] for k in range(8)], axis=0)
        v_ref[8 * half : 8 * half + 8, :] = (pot + y_half)


def local(source_cells, target_cells, source_mass, target_mass, support):
    vmem = pl.BlockSpec(memory_space=pltpu.VMEM)
    hbm = pl.BlockSpec(memory_space=pltpu.HBM)
    u, v = pl.pallas_call(
        kernel,
        out_shape=(
            jax.ShapeDtypeStruct((GROUPS, LANES), jnp.float32),
            jax.ShapeDtypeStruct((GROUPS, LANES), jnp.float32),
        ),
        in_specs=[hbm] * 5,
        out_specs=(vmem, vmem),
        scratch_shapes=[
            pltpu.VMEM((LATENT, 256), jnp.float32),
            pltpu.VMEM((LATENT, LANES), jnp.float32),
            pltpu.VMEM((2, LANES), jnp.float32),
            pltpu.VMEM((1, LANES), jnp.float32),
            pltpu.SMEM((2, 2), jnp.int32),
            pltpu.VMEM((COLS, LANES + 8, LANES), jnp.float32),
            pltpu.VMEM((ROWS, LATENT + 8, LANES), jnp.float32),
            pltpu.VMEM((4, 512, TERMS), jnp.bfloat16),
            pltpu.VMEM((4, TERMS, 512), jnp.bfloat16),
            pltpu.VMEM((GROUPS, 2048, LANES), jnp.float32),
            pltpu.VMEM((2, 4, COLS, 4, LANES), jnp.float32),
            pltpu.VMEM((2, 2, ROWS, 8, LANES), jnp.float32),
            pltpu.VMEM((512, LANES), jnp.float32),
            pltpu.VMEM((2, GROUPS, 8, LANES), jnp.float32),
            pltpu.VMEM((2048, LANES), jnp.float32),
            pltpu.VMEM((2048, LANES), jnp.float32),
            pltpu.VMEM((GROUPS, 8, LANES), jnp.float32),
            pltpu.VMEM((GROUPS, 8, LANES), jnp.float32),
            pltpu.SemaphoreType.DMA((5,)),
            pltpu.SemaphoreType.DMA((7,)),
            pltpu.SemaphoreType.DMA((4,)),
            pltpu.SemaphoreType.DMA((4,)),
            pltpu.SemaphoreType.DMA((4,)),
            pltpu.SemaphoreType.DMA((2, 4)),
            pltpu.SemaphoreType.DMA((2, 2)),
        ],
        compiler_params=pltpu.CompilerParams(
            collective_id=0, has_side_effects=True, vmem_limit_bytes=48 * 1024 * 1024
        ),
        name="sinkhorn",
    )(
        *(
            pltpu.with_memory_space_constraint(value, pltpu.HBM)
            for value in (
                source_cells.T,
                target_cells.T,
                source_mass.reshape(2, LANES),
                target_mass.reshape(1, LANES),
                support,
            )
        )
    )
    return BACK * u.reshape(2048), BACK * v.reshape(2048)


def solution(mesh):
    return jax.shard_map(
        local,
        mesh=mesh,
        in_specs=(
            P(("row", "col"), None),
            P(("col", "row"), None),
            P(("row", "col")),
            P(("col", "row")),
            P("row", "col"),
        ),
        out_specs=(P("row"), P("col")),
        check_vma=False,
    )
```

```python
import math

import jax
import jax.numpy as jnp
from jax import lax
from jax.experimental import pallas as pl
from jax.experimental.pallas import tpu as pltpu
from jax.sharding import PartitionSpec as P

MESH = pl.DeviceIdType.MESH
LATENT = 64
ROWS = 16
COLS = 8
LANES = 128
GROUPS = 16
TERMS = 384
EPSILON = 0.02
NEGATIVE = -1e30
SCALE = math.sqrt(2.0 * math.log2(math.e) / (LATENT * EPSILON))
BACK = EPSILON * math.log(2.0)
FAR_FIRST = tuple(sorted(range(1, ROWS), key=lambda k: -((0, 1, 2, 1)[k & 3] + (0, 1, 2, 1)[k >> 2])))


def pieces(value):
    high = value.astype(jnp.bfloat16)
    rest = value - high.astype(jnp.float32)
    mid = rest.astype(jnp.bfloat16)
    low = (rest - mid.astype(jnp.float32)).astype(jnp.bfloat16)
    return high, mid, low


def tree(op, parts):
    parts = list(parts)
    while len(parts) > 1:
        parts = [
            op(parts[k], parts[k + 1]) if k + 1 < len(parts) else parts[k]
            for k in range(0, len(parts), 2)
        ]
    return parts[0]


def gray(i):
    return i ^ (i // 2)


def kernel(
    x_hbm, y_hbm, a_hbm, b_hbm, support_hbm, u_ref, v_ref,
    x_ref, y_ref, a_ref, b_ref, support_ref,
    xbuf, ybuf, left, right, score, upart, vpart, ucol, vbias,
    row_peak, row_total, col_peak, col_total,
    in_sem, sent, x_recv, relay_recv, y_recv, u_recv, v_recv,
):
    row = lax.axis_index("row")
    col = lax.axis_index("col")
    my_z = row // 4
    my_x = col // 2

    loads = [
        pltpu.make_async_copy(src, dst, in_sem.at[k])
        for k, (src, dst) in enumerate(
            ((x_hbm, x_ref), (y_hbm, y_ref), (a_hbm, a_ref), (b_hbm, b_ref), (support_hbm, support_ref))
        )
    ]
    for load in loads:
        load.start()

    barrier = pltpu.get_barrier_semaphore()
    for k in FAR_FIRST:
        pl.semaphore_signal(barrier, inc=1, device_id=(row ^ k, col), device_id_type=MESH)
    for k in range(1, COLS):
        pl.semaphore_signal(barrier, inc=1, device_id=(row, col ^ k), device_id_type=MESH)

    def bias(a, b):
        return jnp.where(support_ref[a, b] == 1, jnp.float32(0.0), jnp.float32(NEGATIVE))

    def over_row(ref, send, recv, k):
        return pltpu.make_async_remote_copy(
            src_ref=ref.at[row], dst_ref=ref.at[row], send_sem=send, recv_sem=recv,
            device_id=(row ^ k, col), device_id_type=MESH,
        )

    def over_col(ref, send, recv, k):
        return pltpu.make_async_remote_copy(
            src_ref=ref.at[col], dst_ref=ref.at[col], send_sem=send, recv_sem=recv,
            device_id=(row, col ^ k), device_id_type=MESH,
        )

    def relay(owner, k):
        return pltpu.make_async_remote_copy(
            src_ref=xbuf.at[owner], dst_ref=xbuf.at[owner], send_sem=sent.at[1], recv_sem=relay_recv.at[k // 2],
            device_id=(row, col ^ 1), device_id_type=MESH,
        )

    def all_of(ref, sem):
        return pltpu.make_async_copy(ref, ref, sem)

    for load in loads:
        load.wait()
    x_cells = x_ref[...] * SCALE
    x_half = 0.5 * jnp.sum(x_cells * x_cells, axis=0, keepdims=True)
    both = jnp.concatenate([x_cells[:, 0:LANES], x_cells[:, LANES : 2 * LANES]], axis=0)
    xbuf[col, 0:LANES, :] = both.T
    xbuf[col, LANES : LANES + 8, :] = jnp.concatenate(
        [jnp.log2(a_ref[...]), x_half[:, 0:LANES], x_half[:, LANES : 2 * LANES], jnp.zeros((4, LANES), jnp.float32)],
        axis=0,
    )
    y_cells = y_ref[...] * SCALE
    ybuf[row, 0:LATENT, :] = y_cells
    ybuf[row, LATENT : LATENT + 8, :] = jnp.concatenate(
        [
            jnp.log2(b_ref[...]),
            0.5 * jnp.sum(y_cells * y_cells, axis=0, keepdims=True),
            jnp.zeros((6, LANES), jnp.float32),
        ],
        axis=0,
    )

    def clear(i, carry):
        at = pl.ds(pl.multiple_of(i * LANES, LANES), LANES)
        row_peak[at, :] = jnp.full((LANES, LANES), 3.0 * NEGATIVE, jnp.float32)
        row_total[at, :] = jnp.zeros((LANES, LANES), jnp.float32)
        return carry

    lax.fori_loop(0, GROUPS, clear, 0)

    pl.semaphore_wait(barrier, COLS + ROWS - 2)

    for k in (4, 2, 6, 1):
        over_col(xbuf, sent.at[0], x_recv.at[k // 2], k).start()
    for k in (10, 2, 1, 3, 6, 4, 5, 7, 9, 11, 14, 8, 13, 15, 12):
        over_row(ybuf, sent.at[2], y_recv.at[k // 4], k).start()

    lower = lax.broadcasted_iota(jnp.int32, (LANES, LANES), 1) < LATENT
    eye = lax.broadcasted_iota(jnp.int32, (LANES, LANES), 0) == lax.broadcasted_iota(jnp.int32, (LANES, LANES), 1)

    def build_right(level):
        zg = my_z ^ gray(level)
        count = 3 if level == 0 else 4
        all_of(ybuf.at[0:count], y_recv.at[gray(level)]).wait()
        for yy in range(4):
            high, mid, low = pieces(ybuf[zg * 4 + yy, 0:LATENT, :])
            at = slice(yy * LANES, (yy + 1) * LANES)
            for place, piece in enumerate((high, mid, high, mid, low, high)):
                right[zg, LATENT * place : LATENT * (place + 1), at] = piece
            start = -ybuf[zg * 4 + yy, LATENT + 1 : LATENT + 2, :]
            for a in range(2):
                vbias[a, zg * 4 + yy] = jnp.broadcast_to(start + bias(a, zg // 2), (8, LANES))

    def build_left(level):
        xg = my_x ^ gray(level)
        for e in range(2):
            packed = xbuf[2 * xg + e, 0:LANES, :]
            turned = pltpu.roll(packed, LATENT, 1)
            for half in range(2):
                if half == 0:
                    twice = jnp.where(lower, packed, turned)
                else:
                    twice = jnp.where(lower, turned, packed)
                high, mid, low = pieces(twice)
                at = slice((2 * e + half) * LANES, (2 * e + half + 1) * LANES)
                left[xg, at, 0:LANES] = high
                left[xg, at, LANES : 2 * LANES] = mid
                left[xg, at, 2 * LANES : 3 * LANES] = jnp.where(
                    lower, high.astype(jnp.float32), low.astype(jnp.float32)
                ).astype(jnp.bfloat16)

    def tile(xg, zgs):
        pot = [vbias[xg // 2, zg * 4 + c] for zg in zgs for c in range(4)]
        base = xg * 512
        for i in range(4):
            found = []
            for zg in zgs:
                res = jnp.dot(
                    left[xg, i * LANES : (i + 1) * LANES, :], right[zg], preferred_element_type=jnp.float32
                )
                for c in range(4):
                    found.append(res[:, c * LANES : (c + 1) * LANES])
                    at = pl.ds(pl.multiple_of(base + i * LANES, LANES), LANES)
                    score[zg * 4 + c, at, :] = found[-1]
            for q in range(GROUPS):
                at = pl.ds(pl.multiple_of(base + i * LANES + 8 * q, 8), 8)
                t = [part[8 * q : 8 * q + 8, :] + p for part, p in zip(found, pot)]
                old = row_peak[at, :]
                new = jnp.maximum(tree(jnp.maximum, t), old)
                total = tree(jnp.add, [jnp.exp2(value - new) for value in t])
                row_total[at, :] = row_total[at, :] * jnp.exp2(old - new) + total
                row_peak[at, :] = new

    def finish_rows(step, xg, block, peak, total):
        peak, total = peak.T, total.T
        top = jnp.max(peak, axis=0, keepdims=True)
        whole = jnp.sum(total * jnp.exp2(peak - top), axis=0, keepdims=True)
        upart[step, xg, col, pl.ds(block, 1), :] = top + jnp.log2(whole)

    def send_u(step, xg):
        for k in range(1, COLS):
            over_col(upart.at[step, xg], sent.at[3 + step], u_recv.at[step, xg], k).start()

    for k in (2, 6):
        over_col(xbuf, sent.at[0], x_recv.at[k // 2], k).wait_recv()
        relay(col ^ k, k).start()
    over_col(xbuf, sent.at[0], x_recv.at[0], 1).wait_recv()
    build_left(0)
    over_col(xbuf, sent.at[0], x_recv.at[2], 4).wait_recv()
    relay(col ^ 4, 4).start()
    build_right(0)
    for level in range(4):
        if level > 0:
            k = 2 * gray(level)
            relay(col ^ 1 ^ k, k).wait_recv()
            build_left(level)
        tile(my_x ^ gray(level), [my_z])
    build_right(1)

    def second(xg, carry):
        tile(xg, [my_z ^ 1])
        return carry

    lax.fori_loop(0, 4, second, 0)
    build_right(2)
    build_right(3)

    def last(xg, carry):
        tile(xg, [my_z ^ gray(2), my_z ^ gray(3)])
        for block in range(4):
            at = pl.ds(pl.multiple_of(xg * 512 + block * LANES, LANES), LANES)
            finish_rows(0, xg, block, row_peak[at, :], row_total[at, :])
        send_u(0, xg)
        return carry

    lax.fori_loop(0, 4, last, 0)

    def combine_u(step, xg):
        all_of(upart.at[step, xg, 0 : COLS - 1], u_recv.at[step, xg]).wait()
        parts = [upart[step, xg, k] for k in range(COLS)]
        top = tree(jnp.maximum, parts)
        total = tree(jnp.add, [jnp.exp2(p - top) for p in parts])
        mass = jnp.concatenate([xbuf[2 * xg + e, LANES : LANES + 2, :] for e in range(2)], axis=0)
        pot = mass - (top + jnp.log2(total))
        for block in range(4):
            spread = jnp.where(eye, jnp.broadcast_to(pot[block : block + 1, :], (LANES, LANES)), 0.0)
            wide = jnp.sum(spread, axis=1, keepdims=True)
            ucol[block * LANES : (block + 1) * LANES, :] = jnp.broadcast_to(wide, (LANES, LANES))
        if step == 1:
            half = jnp.concatenate([xbuf[2 * xg + e, LANES + 2 : LANES + 4, :] for e in range(2)], axis=0)
            u_ref[pl.ds(xg * 4, 4), :] = (pot + half)

    def column_pass(step):
        col_peak[...] = jnp.full((GROUPS, 8, LANES), 3.0 * NEGATIVE, jnp.float32)
        col_total[...] = jnp.zeros((GROUPS, 8, LANES), jnp.float32)

        def body(t, carry):
            xg, quad = t // 4, t % 4

            @pl.when(quad == 0)
            def _():
                combine_u(step, xg)

            live = bias(xg // 2, quad // 2)
            base = xg * 512
            peaks = [[col_peak[4 * quad + c]] for c in range(4)]
            totals = [[col_total[4 * quad + c]] for c in range(4)]
            for g in range(4):
                pots = [ucol[g * LANES + 8 * k : g * LANES + 8 * k + 8, :] for k in range(GROUPS)]
                for c in range(4):
                    values = [
                        score[4 * quad + c, pl.ds(pl.multiple_of(base + g * LANES + 8 * k, 8), 8), :] + pots[k]
                        for k in range(GROUPS)
                    ]
                    peak = tree(jnp.maximum, values)
                    totals[c].append(tree(jnp.add, [jnp.exp2(value - peak) for value in values]))
                    peaks[c].append(peak + live)
            for c in range(4):
                top = tree(jnp.maximum, peaks[c])
                total = tree(jnp.add, [q * jnp.exp2(p - top) for p, q in zip(peaks[c], totals[c])])
                col_peak[4 * quad + c] = top
                col_total[4 * quad + c] = total

            @pl.when(xg == 3)
            def _():
                lines = []
                for c in range(4):
                    peak, total = col_peak[4 * quad + c], col_total[4 * quad + c]
                    top = jnp.max(peak, axis=0, keepdims=True)
                    whole = jnp.sum(total * jnp.exp2(peak - top), axis=0, keepdims=True)
                    lines.append(top + jnp.log2(whole))
                vpart[step, quad, row] = jnp.concatenate(lines, axis=0)

            @pl.when(xg == 3)
            def _():
                for k in FAR_FIRST:
                    over_row(vpart.at[step, quad], sent.at[5 + step], v_recv.at[step, quad], k).start()

            return carry

        lax.fori_loop(0, GROUPS, body, 0)

    def combine_v(step, half):
        for quad in range(2 * half, 2 * half + 2):
            all_of(vpart.at[step, quad, 0 : ROWS - 1], v_recv.at[step, quad]).wait()
        parts = [
            jnp.concatenate([vpart[step, 2 * half, k], vpart[step, 2 * half + 1, k]], axis=0) for k in range(ROWS)
        ]
        top = tree(jnp.maximum, parts)
        total = tree(jnp.add, [jnp.exp2(p - top) for p in parts])
        mass = jnp.concatenate([ybuf[8 * half + k, LATENT : LATENT + 1, :] for k in range(8)], axis=0)
        return mass - (top + jnp.log2(total))

    column_pass(0)
    for half in range(2):
        pot = combine_v(0, half)
        for a in range(2):
            shifted = pot + bias(a, half)
            for c in range(8):
                vbias[a, 8 * half + c] = jnp.broadcast_to(shifted[c : c + 1, :], (8, LANES))

    def row_block(t, carry):
        xg, block = t // 4, t % 4
        pot = [vbias[xg // 2, c] for c in range(GROUPS)]
        peaks, totals = [], []
        for k in range(GROUPS):
            at = pl.ds(pl.multiple_of(t * LANES + 8 * k, 8), 8)
            values = [score[c, at, :] + pot[c] for c in range(GROUPS)]
            peak = tree(jnp.maximum, values)
            totals.append(tree(jnp.add, [jnp.exp2(value - peak) for value in values]))
            peaks.append(peak)
        finish_rows(1, xg, block, jnp.concatenate(peaks, axis=0), jnp.concatenate(totals, axis=0))

        @pl.when(block == 3)
        def _():
            send_u(1, xg)

        return carry

    lax.fori_loop(0, GROUPS, row_block, 0)
    column_pass(1)
    all_of(xbuf.at[0:4], sent.at[0]).wait()
    all_of(xbuf.at[0:3], sent.at[1]).wait()
    all_of(ybuf.at[0 : ROWS - 1], sent.at[2]).wait()
    for step in range(2):
        all_of(upart.at[step, :, 0 : COLS - 1], sent.at[3 + step]).wait()
        all_of(vpart.at[step, :, 0 : ROWS - 1], sent.at[5 + step]).wait()
    for half in range(2):
        pot = combine_v(1, half)
        y_half = jnp.concatenate([ybuf[8 * half + k, LATENT + 1 : LATENT + 2, :] for k in range(8)], axis=0)
        v_ref[8 * half : 8 * half + 8, :] = (pot + y_half)


def local(source_cells, target_cells, source_mass, target_mass, support):
    vmem = pl.BlockSpec(memory_space=pltpu.VMEM)
    hbm = pl.BlockSpec(memory_space=pltpu.HBM)
    u, v = pl.pallas_call(
        kernel,
        out_shape=(
            jax.ShapeDtypeStruct((GROUPS, LANES), jnp.float32),
            jax.ShapeDtypeStruct((GROUPS, LANES), jnp.float32),
        ),
        in_specs=[hbm] * 5,
        out_specs=(vmem, vmem),
        scratch_shapes=[
            pltpu.VMEM((LATENT, 256), jnp.float32),
            pltpu.VMEM((LATENT, LANES), jnp.float32),
            pltpu.VMEM((2, LANES), jnp.float32),
            pltpu.VMEM((1, LANES), jnp.float32),
            pltpu.SMEM((2, 2), jnp.int32),
            pltpu.VMEM((COLS, LANES + 8, LANES), jnp.float32),
            pltpu.VMEM((ROWS, LATENT + 8, LANES), jnp.float32),
            pltpu.VMEM((4, 512, TERMS), jnp.bfloat16),
            pltpu.VMEM((4, TERMS, 512), jnp.bfloat16),
            pltpu.VMEM((GROUPS, 2048, LANES), jnp.float32),
            pltpu.VMEM((2, 4, COLS, 4, LANES), jnp.float32),
            pltpu.VMEM((2, 4, ROWS, 4, LANES), jnp.float32),
            pltpu.VMEM((512, LANES), jnp.float32),
            pltpu.VMEM((2, GROUPS, 8, LANES), jnp.float32),
            pltpu.VMEM((2048, LANES), jnp.float32),
            pltpu.VMEM((2048, LANES), jnp.float32),
            pltpu.VMEM((GROUPS, 8, LANES), jnp.float32),
            pltpu.VMEM((GROUPS, 8, LANES), jnp.float32),
            pltpu.SemaphoreType.DMA((5,)),
            pltpu.SemaphoreType.DMA((7,)),
            pltpu.SemaphoreType.DMA((4,)),
            pltpu.SemaphoreType.DMA((4,)),
            pltpu.SemaphoreType.DMA((4,)),
            pltpu.SemaphoreType.DMA((2, 4)),
            pltpu.SemaphoreType.DMA((2, 4)),
        ],
        compiler_params=pltpu.CompilerParams(
            collective_id=0, has_side_effects=True, vmem_limit_bytes=48 * 1024 * 1024
        ),
        name="sinkhorn",
    )(
        *(
            pltpu.with_memory_space_constraint(value, pltpu.HBM)
            for value in (
                source_cells.T,
                target_cells.T,
                source_mass.reshape(2, LANES),
                target_mass.reshape(1, LANES),
                support,
            )
        )
    )
    return BACK * u.reshape(2048), BACK * v.reshape(2048)


def solution(mesh):
    return jax.shard_map(
        local,
        mesh=mesh,
        in_specs=(
            P(("row", "col"), None),
            P(("col", "row"), None),
            P(("row", "col")),
            P(("col", "row")),
            P("row", "col"),
        ),
        out_specs=(P("row"), P("col")),
        check_vma=False,
    )
```

```python
import math

import jax
import jax.numpy as jnp
from jax import lax
from jax.experimental import pallas as pl
from jax.experimental.pallas import tpu as pltpu
from jax.sharding import PartitionSpec as P

MESH = pl.DeviceIdType.MESH
LATENT = 64
ROWS = 16
COLS = 8
LANES = 128
GROUPS = 16
TERMS = 384
EPSILON = 0.02
NEGATIVE = -1e30
SCALE = math.sqrt(2.0 * math.log2(math.e) / (LATENT * EPSILON))
BACK = EPSILON * math.log(2.0)
FAR_FIRST = tuple(sorted(range(1, ROWS), key=lambda k: -((0, 1, 2, 1)[k & 3] + (0, 1, 2, 1)[k >> 2])))


def pieces(value):
    high = value.astype(jnp.bfloat16)
    rest = value - high.astype(jnp.float32)
    mid = rest.astype(jnp.bfloat16)
    low = (rest - mid.astype(jnp.float32)).astype(jnp.bfloat16)
    return high, mid, low


def tree(op, parts):
    parts = list(parts)
    while len(parts) > 1:
        parts = [
            op(parts[k], parts[k + 1]) if k + 1 < len(parts) else parts[k]
            for k in range(0, len(parts), 2)
        ]
    return parts[0]


def gray(i):
    return i ^ (i // 2)


def kernel(
    x_hbm, y_hbm, a_hbm, b_hbm, support_hbm, u_ref, v_ref,
    x_ref, y_ref, a_ref, b_ref, support_ref,
    xbuf, ybuf, left, right, score, upart, vpart, ucol, vbias,
    row_peak, row_total, col_peak, col_total,
    in_sem, sent, x_recv, relay_recv, y_recv, u_recv, v_recv,
):
    row = lax.axis_index("row")
    col = lax.axis_index("col")
    my_z = row // 4
    my_x = col // 2

    loads = [
        pltpu.make_async_copy(src, dst, in_sem.at[k])
        for k, (src, dst) in enumerate(
            ((x_hbm, x_ref), (y_hbm, y_ref), (a_hbm, a_ref), (b_hbm, b_ref), (support_hbm, support_ref))
        )
    ]

    barrier = pltpu.get_barrier_semaphore()
    for k in FAR_FIRST:
        pl.semaphore_signal(barrier, inc=1, device_id=(row ^ k, col), device_id_type=MESH)
    for k in range(1, COLS):
        pl.semaphore_signal(barrier, inc=1, device_id=(row, col ^ k), device_id_type=MESH)

    for load in loads:
        load.start()

    def bias(a, b):
        return jnp.where(support_ref[a, b] == 1, jnp.float32(0.0), jnp.float32(NEGATIVE))

    def over_row(ref, send, recv, k):
        return pltpu.make_async_remote_copy(
            src_ref=ref.at[row], dst_ref=ref.at[row], send_sem=send, recv_sem=recv,
            device_id=(row ^ k, col), device_id_type=MESH,
        )

    def over_col(ref, send, recv, k):
        return pltpu.make_async_remote_copy(
            src_ref=ref.at[col], dst_ref=ref.at[col], send_sem=send, recv_sem=recv,
            device_id=(row, col ^ k), device_id_type=MESH,
        )

    def relay(owner, k):
        return pltpu.make_async_remote_copy(
            src_ref=xbuf.at[owner], dst_ref=xbuf.at[owner], send_sem=sent.at[1], recv_sem=relay_recv.at[k // 2],
            device_id=(row, col ^ 1), device_id_type=MESH,
        )

    def all_of(ref, sem):
        return pltpu.make_async_copy(ref, ref, sem)

    for load in loads:
        load.wait()
    x_cells = x_ref[...] * SCALE
    x_half = 0.5 * jnp.sum(x_cells * x_cells, axis=0, keepdims=True)
    both = jnp.concatenate([x_cells[:, 0:LANES], x_cells[:, LANES : 2 * LANES]], axis=0)
    xbuf[col, 0:LANES, :] = both.T
    xbuf[col, LANES : LANES + 8, :] = jnp.concatenate(
        [jnp.log2(a_ref[...]), x_half[:, 0:LANES], x_half[:, LANES : 2 * LANES], jnp.zeros((4, LANES), jnp.float32)],
        axis=0,
    )
    y_cells = y_ref[...] * SCALE
    ybuf[row, 0:LATENT, :] = y_cells
    ybuf[row, LATENT : LATENT + 8, :] = jnp.concatenate(
        [
            jnp.log2(b_ref[...]),
            0.5 * jnp.sum(y_cells * y_cells, axis=0, keepdims=True),
            jnp.zeros((6, LANES), jnp.float32),
        ],
        axis=0,
    )

    def clear(i, carry):
        at = pl.ds(pl.multiple_of(i * LANES, LANES), LANES)
        row_peak[at, :] = jnp.full((LANES, LANES), 3.0 * NEGATIVE, jnp.float32)
        row_total[at, :] = jnp.zeros((LANES, LANES), jnp.float32)
        return carry

    lax.fori_loop(0, GROUPS, clear, 0)

    pl.semaphore_wait(barrier, COLS + ROWS - 2)

    for k in (4, 2, 6, 1):
        over_col(xbuf, sent.at[0], x_recv.at[k // 2], k).start()
    for k in (10, 2, 1, 3, 6, 4, 5, 7, 9, 11, 14, 8, 13, 15, 12):
        over_row(ybuf, sent.at[2], y_recv.at[k // 4], k).start()

    lower = lax.broadcasted_iota(jnp.int32, (LANES, LANES), 1) < LATENT
    eye = lax.broadcasted_iota(jnp.int32, (LANES, LANES), 0) == lax.broadcasted_iota(jnp.int32, (LANES, LANES), 1)

    def build_right(level):
        zg = my_z ^ gray(level)
        count = 3 if level == 0 else 4
        all_of(ybuf.at[0:count], y_recv.at[gray(level)]).wait()
        for yy in range(4):
            high, mid, low = pieces(ybuf[zg * 4 + yy, 0:LATENT, :])
            at = slice(yy * LANES, (yy + 1) * LANES)
            for place, piece in enumerate((high, mid, high, mid, low, high)):
                right[zg, LATENT * place : LATENT * (place + 1), at] = piece
            start = -ybuf[zg * 4 + yy, LATENT + 1 : LATENT + 2, :]
            for a in range(2):
                vbias[a, zg * 4 + yy] = jnp.broadcast_to(start + bias(a, zg // 2), (8, LANES))

    def build_left(level):
        xg = my_x ^ gray(level)
        for e in range(2):
            packed = xbuf[2 * xg + e, 0:LANES, :]
            turned = pltpu.roll(packed, LATENT, 1)
            for half in range(2):
                if half == 0:
                    twice = jnp.where(lower, packed, turned)
                else:
                    twice = jnp.where(lower, turned, packed)
                high, mid, low = pieces(twice)
                at = slice((2 * e + half) * LANES, (2 * e + half + 1) * LANES)
                left[xg, at, 0:LANES] = high
                left[xg, at, LANES : 2 * LANES] = mid
                left[xg, at, 2 * LANES : 3 * LANES] = jnp.where(
                    lower, high.astype(jnp.float32), low.astype(jnp.float32)
                ).astype(jnp.bfloat16)

    def finish_rows(step, xg, block, peak, total):
        peak, total = peak.T, total.T
        top = jnp.max(peak, axis=0, keepdims=True)
        whole = jnp.sum(total * jnp.exp2(peak - top), axis=0, keepdims=True)
        upart[step, xg, col, pl.ds(block, 1), :] = top + jnp.log2(whole)

    def tile(xg, zgs, ending=False):
        pot = [vbias[xg // 2, zg * 4 + c] for zg in zgs for c in range(4)]
        base = xg * 512
        for i in range(4):
            found, peaks, totals = [], [], []
            for zg in zgs:
                res = jnp.dot(
                    left[xg, i * LANES : (i + 1) * LANES, :], right[zg], preferred_element_type=jnp.float32
                )
                for c in range(4):
                    found.append(res[:, c * LANES : (c + 1) * LANES])
                    at = pl.ds(pl.multiple_of(base + i * LANES, LANES), LANES)
                    score[zg * 4 + c, at, :] = found[-1]
            for q in range(GROUPS):
                at = pl.ds(pl.multiple_of(base + i * LANES + 8 * q, 8), 8)
                t = [part[8 * q : 8 * q + 8, :] + p for part, p in zip(found, pot)]
                old = row_peak[at, :]
                new = jnp.maximum(tree(jnp.maximum, t), old)
                total = tree(jnp.add, [jnp.exp2(value - new) for value in t])
                total = row_total[at, :] * jnp.exp2(old - new) + total
                if ending:
                    peaks.append(new)
                    totals.append(total)
                else:
                    row_total[at, :] = total
                    row_peak[at, :] = new
            if ending:
                finish_rows(0, xg, i, jnp.concatenate(peaks, axis=0), jnp.concatenate(totals, axis=0))

    def send_u(step, xg):
        for k in (4, 5, 2, 3, 6, 7, 1):
            over_col(upart.at[step, xg], sent.at[3 + step], u_recv.at[step, xg], k).start()

    for k in (2, 6):
        over_col(xbuf, sent.at[0], x_recv.at[k // 2], k).wait_recv()
        relay(col ^ k, k).start()
    over_col(xbuf, sent.at[0], x_recv.at[0], 1).wait_recv()
    build_left(0)
    over_col(xbuf, sent.at[0], x_recv.at[2], 4).wait_recv()
    relay(col ^ 4, 4).start()
    build_right(0)
    for level in range(4):
        if level > 0:
            k = 2 * gray(level)
            relay(col ^ 1 ^ k, k).wait_recv()
            build_left(level)
        tile(my_x ^ gray(level), [my_z])
    build_right(1)

    def second(xg, carry):
        tile(xg, [my_z ^ 1])
        return carry

    lax.fori_loop(0, 4, second, 0)
    build_right(2)
    build_right(3)

    def last(xg, carry):
        tile(xg, [my_z ^ gray(2), my_z ^ gray(3)], ending=True)
        send_u(0, xg)
        return carry

    lax.fori_loop(0, 4, last, 0)

    def combine_u(step, xg):
        all_of(upart.at[step, xg, 0 : COLS - 1], u_recv.at[step, xg]).wait()
        parts = [upart[step, xg, k] for k in range(COLS)]
        top = tree(jnp.maximum, parts)
        total = tree(jnp.add, [jnp.exp2(p - top) for p in parts])
        mass = jnp.concatenate([xbuf[2 * xg + e, LANES : LANES + 2, :] for e in range(2)], axis=0)
        pot = mass - (top + jnp.log2(total))
        for block in range(4):
            spread = jnp.where(eye, jnp.broadcast_to(pot[block : block + 1, :], (LANES, LANES)), 0.0)
            wide = jnp.sum(spread, axis=1, keepdims=True)
            ucol[block * LANES : (block + 1) * LANES, :] = jnp.broadcast_to(wide, (LANES, LANES))
        if step == 1:
            half = jnp.concatenate([xbuf[2 * xg + e, LANES + 2 : LANES + 4, :] for e in range(2)], axis=0)
            u_ref[pl.ds(xg * 4, 4), :] = (pot + half)

    def column_pass(step):
        col_peak[...] = jnp.full((GROUPS, 8, LANES), 3.0 * NEGATIVE, jnp.float32)
        col_total[...] = jnp.zeros((GROUPS, 8, LANES), jnp.float32)

        def quad_pass(xg, quad):
            live = bias(xg // 2, quad // 2)
            base = xg * 512
            peaks = [[col_peak[4 * quad + c]] for c in range(4)]
            totals = [[col_total[4 * quad + c]] for c in range(4)]
            for g in range(4):
                pots = [ucol[g * LANES + 8 * k : g * LANES + 8 * k + 8, :] for k in range(GROUPS)]
                for c in range(4):
                    values = [
                        score[4 * quad + c, pl.ds(pl.multiple_of(base + g * LANES + 8 * k, 8), 8), :] + pots[k]
                        for k in range(GROUPS)
                    ]
                    peak = tree(jnp.maximum, values)
                    totals[c].append(tree(jnp.add, [jnp.exp2(value - peak) for value in values]))
                    peaks[c].append(peak + live)
            tops = [tree(jnp.maximum, peaks[c]) for c in range(4)]
            sums = [
                tree(jnp.add, [q * jnp.exp2(p - tops[c]) for p, q in zip(peaks[c], totals[c])]) for c in range(4)
            ]
            return tops, sums

        def body(xg, carry):
            combine_u(step, xg)
            for quad in range(4):
                tops, sums = quad_pass(xg, quad)
                for c in range(4):
                    col_peak[4 * quad + c] = tops[c]
                    col_total[4 * quad + c] = sums[c]
            return carry

        lax.fori_loop(0, 3, body, 0)
        combine_u(step, 3)
        for quad in range(4):
            tops, sums = quad_pass(3, quad)
            lines = []
            for peak, total in zip(tops, sums):
                top = jnp.max(peak, axis=0, keepdims=True)
                whole = jnp.sum(total * jnp.exp2(peak - top), axis=0, keepdims=True)
                lines.append(top + jnp.log2(whole))
            vpart[step, quad, row] = jnp.concatenate(lines, axis=0)
            for k in FAR_FIRST:
                over_row(vpart.at[step, quad], sent.at[5 + step], v_recv.at[step, quad], k).start()

    def combine_v(step, half):
        for quad in range(2 * half, 2 * half + 2):
            all_of(vpart.at[step, quad, 0 : ROWS - 1], v_recv.at[step, quad]).wait()
        parts = [
            jnp.concatenate([vpart[step, 2 * half, k], vpart[step, 2 * half + 1, k]], axis=0) for k in range(ROWS)
        ]
        top = tree(jnp.maximum, parts)
        total = tree(jnp.add, [jnp.exp2(p - top) for p in parts])
        mass = jnp.concatenate([ybuf[8 * half + k, LATENT : LATENT + 1, :] for k in range(8)], axis=0)
        return mass - (top + jnp.log2(total))

    column_pass(0)
    for half in range(2):
        pot = combine_v(0, half)
        for a in range(2):
            shifted = pot + bias(a, half)
            for c in range(8):
                vbias[a, 8 * half + c] = jnp.broadcast_to(shifted[c : c + 1, :], (8, LANES))

    def row_blocks(xg, carry):
        for block in range(4):
            pot = [vbias[xg // 2, c] for c in range(GROUPS)]
            peaks, totals = [], []
            for k in range(GROUPS):
                at = pl.ds(pl.multiple_of(xg * 512 + block * LANES + 8 * k, 8), 8)
                values = [score[c, at, :] + pot[c] for c in range(GROUPS)]
                peaks.append(tree(jnp.maximum, values))
                totals.append(tree(jnp.add, [jnp.exp2(value - peaks[-1]) for value in values]))
            finish_rows(1, xg, block, jnp.concatenate(peaks, axis=0), jnp.concatenate(totals, axis=0))
        send_u(1, xg)
        return carry

    lax.fori_loop(0, 4, row_blocks, 0)
    column_pass(1)
    all_of(xbuf.at[0:4], sent.at[0]).wait()
    all_of(xbuf.at[0:3], sent.at[1]).wait()
    all_of(ybuf.at[0 : ROWS - 1], sent.at[2]).wait()
    for step in range(2):
        all_of(upart.at[step, :, 0 : COLS - 1], sent.at[3 + step]).wait()
        all_of(vpart.at[step, :, 0 : ROWS - 1], sent.at[5 + step]).wait()
    for half in range(2):
        pot = combine_v(1, half)
        y_half = jnp.concatenate([ybuf[8 * half + k, LATENT + 1 : LATENT + 2, :] for k in range(8)], axis=0)
        v_ref[8 * half : 8 * half + 8, :] = (pot + y_half)


def local(source_cells, target_cells, source_mass, target_mass, support):
    vmem = pl.BlockSpec(memory_space=pltpu.VMEM)
    hbm = pl.BlockSpec(memory_space=pltpu.HBM)
    u, v = pl.pallas_call(
        kernel,
        out_shape=(
            jax.ShapeDtypeStruct((GROUPS, LANES), jnp.float32),
            jax.ShapeDtypeStruct((GROUPS, LANES), jnp.float32),
        ),
        in_specs=[hbm] * 5,
        out_specs=(vmem, vmem),
        scratch_shapes=[
            pltpu.VMEM((LATENT, 256), jnp.float32),
            pltpu.VMEM((LATENT, LANES), jnp.float32),
            pltpu.VMEM((2, LANES), jnp.float32),
            pltpu.VMEM((1, LANES), jnp.float32),
            pltpu.SMEM((2, 2), jnp.int32),
            pltpu.VMEM((COLS, LANES + 8, LANES), jnp.float32),
            pltpu.VMEM((ROWS, LATENT + 8, LANES), jnp.float32),
            pltpu.VMEM((4, 512, TERMS), jnp.bfloat16),
            pltpu.VMEM((4, TERMS, 512), jnp.bfloat16),
            pltpu.VMEM((GROUPS, 2048, LANES), jnp.float32),
            pltpu.VMEM((2, 4, COLS, 4, LANES), jnp.float32),
            pltpu.VMEM((2, 4, ROWS, 4, LANES), jnp.float32),
            pltpu.VMEM((512, LANES), jnp.float32),
            pltpu.VMEM((2, GROUPS, 8, LANES), jnp.float32),
            pltpu.VMEM((2048, LANES), jnp.float32),
            pltpu.VMEM((2048, LANES), jnp.float32),
            pltpu.VMEM((GROUPS, 8, LANES), jnp.float32),
            pltpu.VMEM((GROUPS, 8, LANES), jnp.float32),
            pltpu.SemaphoreType.DMA((5,)),
            pltpu.SemaphoreType.DMA((7,)),
            pltpu.SemaphoreType.DMA((4,)),
            pltpu.SemaphoreType.DMA((4,)),
            pltpu.SemaphoreType.DMA((4,)),
            pltpu.SemaphoreType.DMA((2, 4)),
            pltpu.SemaphoreType.DMA((2, 4)),
        ],
        compiler_params=pltpu.CompilerParams(
            collective_id=0, has_side_effects=True, vmem_limit_bytes=48 * 1024 * 1024
        ),
        name="sinkhorn",
    )(
        *(
            pltpu.with_memory_space_constraint(value, pltpu.HBM)
            for value in (
                source_cells.T,
                target_cells.T,
                source_mass.reshape(2, LANES),
                target_mass.reshape(1, LANES),
                support,
            )
        )
    )
    return BACK * u.reshape(2048), BACK * v.reshape(2048)


def solution(mesh):
    return jax.shard_map(
        local,
        mesh=mesh,
        in_specs=(
            P(("row", "col"), None),
            P(("col", "row"), None),
            P(("row", "col")),
            P(("col", "row")),
            P("row", "col"),
        ),
        out_specs=(P("row"), P("col")),
        check_vma=False,
    )
```

```python
import math

import jax
import jax.numpy as jnp
from jax import lax
from jax.experimental import pallas as pl
from jax.experimental.pallas import tpu as pltpu
from jax.sharding import PartitionSpec as P

MESH = pl.DeviceIdType.MESH
LATENT = 64
ROWS = 16
COLS = 8
LANES = 128
GROUPS = 16
TERMS = 384
EPSILON = 0.02
NEGATIVE = -1e30
SCALE = math.sqrt(2.0 * math.log2(math.e) / (LATENT * EPSILON))
BACK = EPSILON * math.log(2.0)
FAR_FIRST = tuple(sorted(range(1, ROWS), key=lambda k: -((0, 1, 2, 1)[k & 3] + (0, 1, 2, 1)[k >> 2])))


def pieces(value):
    high = value.astype(jnp.bfloat16)
    rest = value - high.astype(jnp.float32)
    mid = rest.astype(jnp.bfloat16)
    low = (rest - mid.astype(jnp.float32)).astype(jnp.bfloat16)
    return high, mid, low


def tree(op, parts):
    parts = list(parts)
    while len(parts) > 1:
        parts = [
            op(parts[k], parts[k + 1]) if k + 1 < len(parts) else parts[k]
            for k in range(0, len(parts), 2)
        ]
    return parts[0]


def gray(i):
    return i ^ (i // 2)


def kernel(
    x_hbm, y_hbm, a_hbm, b_hbm, support_hbm, u_ref, v_ref,
    x_ref, y_ref, a_ref, b_ref, support_ref,
    xbuf, ybuf, left, right, score, upart, vpart, ucol, vbias,
    row_peak, row_total, col_peak, col_total,
    in_sem, sent, x_recv, relay_recv, y_recv, u_recv, v_recv,
):
    row = lax.axis_index("row")
    col = lax.axis_index("col")
    my_z = row // 4
    my_x = col // 2

    loads = [
        pltpu.make_async_copy(src, dst, in_sem.at[k])
        for k, (src, dst) in enumerate(
            ((x_hbm, x_ref), (y_hbm, y_ref), (a_hbm, a_ref), (b_hbm, b_ref), (support_hbm, support_ref))
        )
    ]

    barrier = pltpu.get_barrier_semaphore()
    for k in FAR_FIRST:
        pl.semaphore_signal(barrier, inc=1, device_id=(row ^ k, col), device_id_type=MESH)
    for k in range(1, COLS):
        pl.semaphore_signal(barrier, inc=1, device_id=(row, col ^ k), device_id_type=MESH)

    for load in loads:
        load.start()

    def bias(a, b):
        return jnp.where(support_ref[a, b] == 1, jnp.float32(0.0), jnp.float32(NEGATIVE))

    def over_row(ref, send, recv, k):
        return pltpu.make_async_remote_copy(
            src_ref=ref.at[row], dst_ref=ref.at[row], send_sem=send, recv_sem=recv,
            device_id=(row ^ k, col), device_id_type=MESH,
        )

    def over_col(ref, send, recv, k):
        return pltpu.make_async_remote_copy(
            src_ref=ref.at[col], dst_ref=ref.at[col], send_sem=send, recv_sem=recv,
            device_id=(row, col ^ k), device_id_type=MESH,
        )

    def relay(owner, k):
        return pltpu.make_async_remote_copy(
            src_ref=xbuf.at[owner], dst_ref=xbuf.at[owner], send_sem=sent.at[1], recv_sem=relay_recv.at[k // 2],
            device_id=(row, col ^ 1), device_id_type=MESH,
        )

    def all_of(ref, sem):
        return pltpu.make_async_copy(ref, ref, sem)

    for load in loads:
        load.wait()
    x_cells = x_ref[...] * SCALE
    x_half = 0.5 * jnp.sum(x_cells * x_cells, axis=0, keepdims=True)
    both = jnp.concatenate([x_cells[:, 0:LANES], x_cells[:, LANES : 2 * LANES]], axis=0)
    xbuf[col, 0:LANES, :] = both.T
    xbuf[col, LANES : LANES + 8, :] = jnp.concatenate(
        [jnp.log2(a_ref[...]), x_half[:, 0:LANES], x_half[:, LANES : 2 * LANES], jnp.zeros((4, LANES), jnp.float32)],
        axis=0,
    )
    y_cells = y_ref[...] * SCALE
    ybuf[row, 0:LATENT, :] = y_cells
    ybuf[row, LATENT : LATENT + 8, :] = jnp.concatenate(
        [
            jnp.log2(b_ref[...]),
            0.5 * jnp.sum(y_cells * y_cells, axis=0, keepdims=True),
            jnp.zeros((6, LANES), jnp.float32),
        ],
        axis=0,
    )

    def clear(i, carry):
        at = pl.ds(pl.multiple_of(i * LANES, LANES), LANES)
        row_peak[at, :] = jnp.full((LANES, LANES), 3.0 * NEGATIVE, jnp.float32)
        row_total[at, :] = jnp.zeros((LANES, LANES), jnp.float32)
        return carry

    lax.fori_loop(0, GROUPS, clear, 0)

    pl.semaphore_wait(barrier, COLS + ROWS - 2)

    for k in (4, 2, 6, 1):
        over_col(xbuf, sent.at[0], x_recv.at[k // 2], k).start()
    for k in (10, 2, 1, 3, 6, 4, 5, 7, 9, 11, 14, 8, 13, 15, 12):
        over_row(ybuf, sent.at[2], y_recv.at[k // 4], k).start()

    lower = lax.broadcasted_iota(jnp.int32, (LANES, LANES), 1) < LATENT
    eye = lax.broadcasted_iota(jnp.int32, (LANES, LANES), 0) == lax.broadcasted_iota(jnp.int32, (LANES, LANES), 1)

    def build_right(level):
        zg = my_z ^ gray(level)
        count = 3 if level == 0 else 4
        all_of(ybuf.at[0:count], y_recv.at[gray(level)]).wait()
        for yy in range(4):
            high, mid, low = pieces(ybuf[zg * 4 + yy, 0:LATENT, :])
            at = slice(yy * LANES, (yy + 1) * LANES)
            for place, piece in enumerate((high, mid, high, mid, low, high)):
                right[zg, LATENT * place : LATENT * (place + 1), at] = piece
            start = -ybuf[zg * 4 + yy, LATENT + 1 : LATENT + 2, :]
            for a in range(2):
                vbias[a, zg * 4 + yy] = jnp.broadcast_to(start + bias(a, zg // 2), (8, LANES))

    def build_left(level):
        xg = my_x ^ gray(level)
        for e in range(2):
            packed = xbuf[2 * xg + e, 0:LANES, :]
            turned = pltpu.roll(packed, LATENT, 1)
            for half in range(2):
                if half == 0:
                    twice = jnp.where(lower, packed, turned)
                else:
                    twice = jnp.where(lower, turned, packed)
                high, mid, low = pieces(twice)
                at = slice((2 * e + half) * LANES, (2 * e + half + 1) * LANES)
                left[xg, at, 0:LANES] = high
                left[xg, at, LANES : 2 * LANES] = mid
                left[xg, at, 2 * LANES : 3 * LANES] = jnp.where(
                    lower, high.astype(jnp.float32), low.astype(jnp.float32)
                ).astype(jnp.bfloat16)

    def finish_rows(step, xg, block, peak, total):
        value = (peak + jnp.log2(total)).T
        top = jnp.max(value, axis=0, keepdims=True)
        whole = jnp.sum(jnp.exp2(value - top), axis=0, keepdims=True)
        upart[step, xg, col, pl.ds(block, 1), :] = top + jnp.log2(whole)

    def tile(xg, zgs, ending=False):
        pot = [vbias[xg // 2, zg * 4 + c] for zg in zgs for c in range(4)]
        base = xg * 512
        for i in range(4):
            found, peaks, totals = [], [], []
            for zg in zgs:
                res = jnp.dot(
                    left[xg, i * LANES : (i + 1) * LANES, :], right[zg], preferred_element_type=jnp.float32
                )
                for c in range(4):
                    found.append(res[:, c * LANES : (c + 1) * LANES])
                    at = pl.ds(pl.multiple_of(base + i * LANES, LANES), LANES)
                    score[zg * 4 + c, at, :] = found[-1]
            for q in range(GROUPS):
                at = pl.ds(pl.multiple_of(base + i * LANES + 8 * q, 8), 8)
                t = [part[8 * q : 8 * q + 8, :] + p for part, p in zip(found, pot)]
                old = row_peak[at, :]
                new = jnp.maximum(tree(jnp.maximum, t), old)
                total = tree(jnp.add, [jnp.exp2(value - new) for value in t])
                total = row_total[at, :] * jnp.exp2(old - new) + total
                if ending:
                    peaks.append(new)
                    totals.append(total)
                else:
                    row_total[at, :] = total
                    row_peak[at, :] = new
            if ending:
                finish_rows(0, xg, i, jnp.concatenate(peaks, axis=0), jnp.concatenate(totals, axis=0))

    def send_u(step, xg):
        for k in (4, 5, 2, 3, 6, 7, 1):
            over_col(upart.at[step, xg], sent.at[3 + step], u_recv.at[step, xg], k).start()

    for k in (2, 6):
        over_col(xbuf, sent.at[0], x_recv.at[k // 2], k).wait_recv()
        relay(col ^ k, k).start()
    over_col(xbuf, sent.at[0], x_recv.at[0], 1).wait_recv()
    build_left(0)
    over_col(xbuf, sent.at[0], x_recv.at[2], 4).wait_recv()
    relay(col ^ 4, 4).start()
    build_right(0)
    for level in range(4):
        if level > 0:
            k = 2 * gray(level)
            relay(col ^ 1 ^ k, k).wait_recv()
            build_left(level)
        tile(my_x ^ gray(level), [my_z])
    build_right(1)

    def second(xg, carry):
        tile(xg, [my_z ^ 1])
        return carry

    lax.fori_loop(0, 4, second, 0)
    build_right(2)
    build_right(3)

    def last(xg, carry):
        tile(xg, [my_z ^ gray(2), my_z ^ gray(3)], ending=True)
        send_u(0, xg)
        return carry

    lax.fori_loop(0, 4, last, 0)

    def combine_u(step, xg):
        all_of(upart.at[step, xg, 0 : COLS - 1], u_recv.at[step, xg]).wait()
        parts = [upart[step, xg, k] for k in range(COLS)]
        top = tree(jnp.maximum, parts)
        total = tree(jnp.add, [jnp.exp2(p - top) for p in parts])
        mass = jnp.concatenate([xbuf[2 * xg + e, LANES : LANES + 2, :] for e in range(2)], axis=0)
        pot = mass - (top + jnp.log2(total))
        for block in range(4):
            spread = jnp.where(eye, jnp.broadcast_to(pot[block : block + 1, :], (LANES, LANES)), 0.0)
            wide = jnp.sum(spread, axis=1, keepdims=True)
            ucol[block * LANES : (block + 1) * LANES, :] = jnp.broadcast_to(wide, (LANES, LANES))
        if step == 1:
            half = jnp.concatenate([xbuf[2 * xg + e, LANES + 2 : LANES + 4, :] for e in range(2)], axis=0)
            u_ref[pl.ds(xg * 4, 4), :] = (pot + half)

    def column_pass(step):
        col_peak[...] = jnp.full((GROUPS, 8, LANES), 3.0 * NEGATIVE, jnp.float32)
        col_total[...] = jnp.zeros((GROUPS, 8, LANES), jnp.float32)

        def quad_pass(xg, quad):
            live = bias(xg // 2, quad // 2)
            base = xg * 512
            peaks = [[col_peak[4 * quad + c]] for c in range(4)]
            totals = [[col_total[4 * quad + c]] for c in range(4)]
            for g in range(4):
                pots = [ucol[g * LANES + 8 * k : g * LANES + 8 * k + 8, :] for k in range(GROUPS)]
                for c in range(4):
                    values = [
                        score[4 * quad + c, pl.ds(pl.multiple_of(base + g * LANES + 8 * k, 8), 8), :] + pots[k]
                        for k in range(GROUPS)
                    ]
                    peak = tree(jnp.maximum, values)
                    totals[c].append(tree(jnp.add, [jnp.exp2(value - peak) for value in values]))
                    peaks[c].append(peak + live)
            tops = [tree(jnp.maximum, peaks[c]) for c in range(4)]
            sums = [
                tree(jnp.add, [q * jnp.exp2(p - tops[c]) for p, q in zip(peaks[c], totals[c])]) for c in range(4)
            ]
            return tops, sums

        def body(xg, carry):
            combine_u(step, xg)
            for quad in range(4):
                tops, sums = quad_pass(xg, quad)
                for c in range(4):
                    col_peak[4 * quad + c] = tops[c]
                    col_total[4 * quad + c] = sums[c]
            return carry

        lax.fori_loop(0, 3, body, 0)
        combine_u(step, 3)
        for quad in range(4):
            tops, sums = quad_pass(3, quad)
            lines = []
            for peak, total in zip(tops, sums):
                top = jnp.max(peak, axis=0, keepdims=True)
                whole = jnp.sum(total * jnp.exp2(peak - top), axis=0, keepdims=True)
                lines.append(top + jnp.log2(whole))
            vpart[step, quad, row] = jnp.concatenate(lines, axis=0)
            for k in FAR_FIRST:
                over_row(vpart.at[step, quad], sent.at[5 + step], v_recv.at[step, quad], k).start()

    def combine_v(step, half):
        for quad in range(2 * half, 2 * half + 2):
            all_of(vpart.at[step, quad, 0 : ROWS - 1], v_recv.at[step, quad]).wait()
        parts = [
            jnp.concatenate([vpart[step, 2 * half, k], vpart[step, 2 * half + 1, k]], axis=0) for k in range(ROWS)
        ]
        top = tree(jnp.maximum, parts)
        total = tree(jnp.add, [jnp.exp2(p - top) for p in parts])
        mass = jnp.concatenate([ybuf[8 * half + k, LATENT : LATENT + 1, :] for k in range(8)], axis=0)
        return mass - (top + jnp.log2(total))

    column_pass(0)
    for half in range(2):
        pot = combine_v(0, half)
        for a in range(2):
            shifted = pot + bias(a, half)
            for c in range(8):
                vbias[a, 8 * half + c] = jnp.broadcast_to(shifted[c : c + 1, :], (8, LANES))

    def row_blocks(xg, carry):
        for block in range(4):
            pot = [vbias[xg // 2, c] for c in range(GROUPS)]
            peaks, totals = [], []
            for k in range(GROUPS):
                at = pl.ds(pl.multiple_of(xg * 512 + block * LANES + 8 * k, 8), 8)
                values = [score[c, at, :] + pot[c] for c in range(GROUPS)]
                peaks.append(tree(jnp.maximum, values))
                totals.append(tree(jnp.add, [jnp.exp2(value - peaks[-1]) for value in values]))
            finish_rows(1, xg, block, jnp.concatenate(peaks, axis=0), jnp.concatenate(totals, axis=0))
        send_u(1, xg)
        return carry

    lax.fori_loop(0, 4, row_blocks, 0)
    column_pass(1)
    all_of(xbuf.at[0:4], sent.at[0]).wait()
    all_of(xbuf.at[0:3], sent.at[1]).wait()
    all_of(ybuf.at[0 : ROWS - 1], sent.at[2]).wait()
    for step in range(2):
        all_of(upart.at[step, :, 0 : COLS - 1], sent.at[3 + step]).wait()
        all_of(vpart.at[step, :, 0 : ROWS - 1], sent.at[5 + step]).wait()
    for half in range(2):
        pot = combine_v(1, half)
        y_half = jnp.concatenate([ybuf[8 * half + k, LATENT + 1 : LATENT + 2, :] for k in range(8)], axis=0)
        v_ref[8 * half : 8 * half + 8, :] = (pot + y_half)


def local(source_cells, target_cells, source_mass, target_mass, support):
    vmem = pl.BlockSpec(memory_space=pltpu.VMEM)
    hbm = pl.BlockSpec(memory_space=pltpu.HBM)
    u, v = pl.pallas_call(
        kernel,
        out_shape=(
            jax.ShapeDtypeStruct((GROUPS, LANES), jnp.float32),
            jax.ShapeDtypeStruct((GROUPS, LANES), jnp.float32),
        ),
        in_specs=[hbm] * 5,
        out_specs=(vmem, vmem),
        scratch_shapes=[
            pltpu.VMEM((LATENT, 256), jnp.float32),
            pltpu.VMEM((LATENT, LANES), jnp.float32),
            pltpu.VMEM((2, LANES), jnp.float32),
            pltpu.VMEM((1, LANES), jnp.float32),
            pltpu.SMEM((2, 2), jnp.int32),
            pltpu.VMEM((COLS, LANES + 8, LANES), jnp.float32),
            pltpu.VMEM((ROWS, LATENT + 8, LANES), jnp.float32),
            pltpu.VMEM((4, 512, TERMS), jnp.bfloat16),
            pltpu.VMEM((4, TERMS, 512), jnp.bfloat16),
            pltpu.VMEM((GROUPS, 2048, LANES), jnp.float32),
            pltpu.VMEM((2, 4, COLS, 4, LANES), jnp.float32),
            pltpu.VMEM((2, 4, ROWS, 4, LANES), jnp.float32),
            pltpu.VMEM((512, LANES), jnp.float32),
            pltpu.VMEM((2, GROUPS, 8, LANES), jnp.float32),
            pltpu.VMEM((2048, LANES), jnp.float32),
            pltpu.VMEM((2048, LANES), jnp.float32),
            pltpu.VMEM((GROUPS, 8, LANES), jnp.float32),
            pltpu.VMEM((GROUPS, 8, LANES), jnp.float32),
            pltpu.SemaphoreType.DMA((5,)),
            pltpu.SemaphoreType.DMA((7,)),
            pltpu.SemaphoreType.DMA((4,)),
            pltpu.SemaphoreType.DMA((4,)),
            pltpu.SemaphoreType.DMA((4,)),
            pltpu.SemaphoreType.DMA((2, 4)),
            pltpu.SemaphoreType.DMA((2, 4)),
        ],
        compiler_params=pltpu.CompilerParams(
            collective_id=0, has_side_effects=True, vmem_limit_bytes=48 * 1024 * 1024
        ),
        name="sinkhorn",
    )(
        *(
            pltpu.with_memory_space_constraint(value, pltpu.HBM)
            for value in (
                source_cells.T,
                target_cells.T,
                source_mass.reshape(2, LANES),
                target_mass.reshape(1, LANES),
                support,
            )
        )
    )
    return BACK * u.reshape(2048), BACK * v.reshape(2048)


def solution(mesh):
    return jax.shard_map(
        local,
        mesh=mesh,
        in_specs=(
            P(("row", "col"), None),
            P(("col", "row"), None),
            P(("row", "col")),
            P(("col", "row")),
            P("row", "col"),
        ),
        out_specs=(P("row"), P("col")),
        check_vma=False,
    )
```
